256 devices in a mesh: tbl: 64 (over z, y, core), tm: 4 (over x).
Axes of the slice: x: 4, y: 4, z: 8, core: 2. Of those that a mesh axis runs over, the one named last changes fastest.
Arguments:
- table: bfloat16 [2097152, 128], P('tbl'), may hold values from -64 to 64
- fetch_rows: int32 [64, 4, 64, 512], P('tbl', 'tm'), may hold values from 0 to 32767
- tile_counts: int32 [64, 4, 64], P('tbl', 'tm'), may hold values from 1 to 4, as said below
- hist_source: int32 [64, 4, 2, 8192], P('tbl', 'tm'), may hold values from 0 to 32767, as said below
- cand_source: int32 [64, 4, 512], P('tbl', 'tm'), may hold values from 0 to 32767, as said below
- lengths: int32 [64, 2], P('tbl'), may hold values from 1 to 32768
- w_query: bfloat16 [128, 128], replicated, may hold values from -0.5 to 0.5
- w_key: bfloat16 [128, 128], replicated, may hold values from -0.5 to 0.5
- w_value: bfloat16 [128, 128], replicated, may hold values from -0.5 to 0.5
- w_out: bfloat16 [128, 128], replicated, may hold values from -0.5 to 0.5
Outputs:
- interest: bfloat16 [131072, 128], P(('tbl', 'tm'))
The draws below stay inside these ranges and needn't reach their ends.
Inputs may be any that keep to these rules, and one draw needn't show every extreme that they name: `tile_counts`: in every draw some owner is asked for 4 tiles by every device, and on every device at least one owner has 4 live tiles. `hist_source`: every entry names a slot in a tile that tile_counts counts live for that device and owner. On every device all 512 slots of some owner are named. `cand_source`: every entry names a slot in a tile that tile_counts counts live for that device and owner.
All inputs are finite; a program needn't handle non-finite values.
Results may differ from the reference program's by a relative error of at most 0.0059.
The reference program's roundings to bfloat16 on the way count: a program that leaves them out, or rounds other values in their place, can miss the bound.
Values may be sent and summed in bfloat16 or wider, within the bound.
A program may use at most 128 MiB of HBM per device.

```python
import math
import jax
import jax.numpy as jnp
from jax import lax

EMBED = 128
HEADS = 4
HEAD_DIM = 32
TILE = 128
TILES_MAX = 4
REQUESTS = 2
SLICE_LEN = 8192
CANDS = 1024
TBL_DEV = 32768
GROUPS = 64
OWNERS = 64
SLICES = 4
CAP = 512
CAND_DEV = 512
MAX_LEN = 32768
TABLE = 2097152
N_TM = 4


def owner_tiles(key):
    base_key = jax.random.fold_in(key, 101)
    counts = jax.random.randint(jax.random.fold_in(base_key, 2), (GROUPS, SLICES, OWNERS), 1, TILES_MAX + 1)
    full_owner = jax.random.randint(jax.random.fold_in(base_key, 3), (GROUPS, SLICES, 1), 0, OWNERS).astype(jnp.int32)
    owner_ids = jnp.arange(OWNERS, dtype=jnp.int32)
    forced = (owner_ids[None, None, :] == OWNERS - 1) | (owner_ids[None, None, :] == full_owner)
    return (jnp.where(forced, TILES_MAX, counts).astype(jnp.int32), full_owner)


def live_slots(counts, key, length):
    ends = jnp.cumsum(counts, axis=-1).astype(jnp.int32)
    starts = ends - counts
    total_tiles = ends[:, :, -1:]
    raw_draw = jax.random.randint(jax.random.fold_in(key, 1), (GROUPS, SLICES, length), 0, 2 ** 30)
    tile_pick = (raw_draw % total_tiles).astype(jnp.int32)
    lane_pick = jax.random.randint(jax.random.fold_in(key, 2), (GROUPS, SLICES, length), 0, TILE)
    finder = jax.vmap(jax.vmap(lambda edges, wanted: jnp.searchsorted(edges, wanted, side='right')))
    owner_pick = finder(ends, tile_pick).astype(jnp.int32)
    owner_start = jnp.take_along_axis(starts, owner_pick, axis=-1)
    slots = (owner_pick * CAP + (tile_pick - owner_start) * TILE + lane_pick).astype(jnp.int32)
    position = jnp.arange(length, dtype=jnp.int32)
    return jnp.where(position[None, None, :] == length - 1, OWNERS * CAP - 1, slots).astype(jnp.int32)


def draw_tile_counts(key, part):
    counts, full_owner = owner_tiles(key)
    return counts


def draw_hist_source(key, part):
    counts, full_owner = owner_tiles(key)
    key = jax.random.fold_in(key, 5)
    length = REQUESTS * SLICE_LEN
    slots = live_slots(counts, key, length)
    position = jnp.arange(length, dtype=jnp.int32)[None, None, :]
    offset = jax.random.randint(jax.random.fold_in(key, 3), (GROUPS, SLICES, 1), 0, CAP).astype(jnp.int32)
    cover = (full_owner * CAP + (position + offset) % CAP).astype(jnp.int32)
    slots = jnp.where(position < CAP, cover, slots).astype(jnp.int32)
    return slots.reshape(GROUPS, SLICES, REQUESTS, SLICE_LEN)


def draw_cand_source(key, part):
    counts, full_owner = owner_tiles(key)
    key = jax.random.fold_in(key, 7)
    return live_slots(counts, key, CAND_DEV)


def draw_table(key, part):
    key = jax.random.fold_in(key, 9)
    values_drawn = jax.random.normal(jax.random.fold_in(key, 1), (TABLE, EMBED), jnp.float32)
    return values_drawn.astype(jnp.bfloat16)


def set_ends(drawn, stream_key, least, largest):
    shape = drawn.shape
    spot = [jax.random.randint(jax.random.fold_in(stream_key, axis), (), 0, shape[axis]) for axis in range(len(shape))]
    drawn = drawn.at[tuple(spot)].set(least)
    longest = shape.index(max(shape))
    spot[longest] = (spot[longest] + 1) % shape[longest]
    return drawn.at[tuple(spot)].set(largest)


def normal_values(key, extent, deviation, limit, kind=jnp.bfloat16):
    array = jax.random.normal(key, extent, jnp.float32) * deviation
    return jnp.minimum(jnp.maximum(array, -limit), limit).astype(kind)


def setup_inputs(seed: int = 0) -> dict:
    streams_of = jax.random.split(jax.random.key(seed), 11)
    table = draw_table(jax.random.fold_in(streams_of[10], 71), 0)
    fetch_rows = set_ends(jax.random.randint(streams_of[1], (GROUPS, SLICES, OWNERS, CAP), 0, TBL_DEV), jax.random.fold_in(streams_of[1], 1), 0, TBL_DEV - 1).astype(jnp.int32)
    tile_counts = draw_tile_counts(jax.random.fold_in(streams_of[10], 71), 0)
    hist_source = draw_hist_source(jax.random.fold_in(streams_of[10], 71), 0)
    cand_source = draw_cand_source(jax.random.fold_in(streams_of[10], 71), 0)
    lengths = set_ends(jax.random.randint(streams_of[5], (GROUPS, REQUESTS), 1, MAX_LEN + 1), jax.random.fold_in(streams_of[5], 1), 1, MAX_LEN).astype(jnp.int32)
    w_query = normal_values(streams_of[6], (EMBED, EMBED), EMBED ** -0.5, 0.5)
    w_key = normal_values(streams_of[7], (EMBED, EMBED), EMBED ** -0.5, 0.5)
    w_value = normal_values(streams_of[8], (EMBED, EMBED), EMBED ** -0.5, 0.5)
    w_out = normal_values(streams_of[9], (EMBED, EMBED), EMBED ** -0.5, 0.5)
    return {"table": table, "fetch_rows": fetch_rows, "tile_counts": tile_counts, "hist_source": hist_source, "cand_source": cand_source, "lengths": lengths, "w_query": w_query, "w_key": w_key, "w_value": w_value, "w_out": w_out}


NEG_FILL = -1e+30

def fetch_slice(table, id_block, count_block):
    owner_base = (jnp.arange(OWNERS, dtype=jnp.int32) * TBL_DEV)[:, None]
    looked = jnp.take(table, (id_block + owner_base).reshape(-1), axis=0).reshape(OWNERS, CAP, EMBED)
    tile_index = jnp.arange(CAP, dtype=jnp.int32) // TILE
    counted = tile_index[None, :] < count_block[:, None]
    looked = jnp.where(counted[:, :, None], looked, jnp.zeros((), looked.dtype))
    return looked.reshape(OWNERS * CAP, EMBED)

def slice_partials(queries, keys_slice, values_slice, live_len):
    score_scale = 1.0 / math.sqrt(HEAD_DIM)

    def per_request(operands):
        query_one, keys_one, values_one, live_one = operands
        scores = jnp.einsum('chd,phd->hcp', query_one.astype(jnp.float32), keys_one.astype(jnp.float32)) * score_scale
        visible = (jnp.arange(SLICE_LEN, dtype=jnp.int32) < live_one)[None, None, :]
        masked = jnp.where(visible, scores, NEG_FILL)
        peak_score = lax.optimization_barrier(jnp.max(masked, axis=2))
        weights = jnp.where(visible, jnp.exp(masked - peak_score[..., None]), 0.0).astype(jnp.bfloat16)
        weight_sum = lax.optimization_barrier(jnp.sum(weights.astype(jnp.float32), axis=2))
        numerators = jnp.einsum('hcp,phd->chd', weights.astype(jnp.float32), values_one.astype(jnp.float32))
        return (peak_score, weight_sum, numerators)
    return lax.map(per_request, (queries, keys_slice, values_slice, live_len))

def reference(table, fetch_rows, tile_counts, hist_source, cand_source, lengths, w_query, w_key, w_value, w_out):

    def one_group(operands):
        id_group, count_group, hist_group, cand_group, length_group = operands
        keys_list = []
        values_list = []
        cand_list = []
        for slice_pos in range(N_TM):
            flat_rows = fetch_slice(table, id_group[slice_pos], count_group[slice_pos])
            history = jnp.take(flat_rows, hist_group[slice_pos].reshape(-1), axis=0)
            keys_here = jnp.dot(history, w_key, preferred_element_type=jnp.float32).astype(jnp.bfloat16)
            values_here = jnp.dot(history, w_value, preferred_element_type=jnp.float32).astype(jnp.bfloat16)
            keys_list.append(keys_here.reshape(REQUESTS, SLICE_LEN, HEADS, HEAD_DIM))
            values_list.append(values_here.reshape(REQUESTS, SLICE_LEN, HEADS, HEAD_DIM))
            cand_list.append(jnp.take(flat_rows, cand_group[slice_pos], axis=0))
        cand_embed = jnp.concatenate(cand_list, axis=0)
        queries = jnp.dot(cand_embed, w_query, preferred_element_type=jnp.float32).astype(jnp.bfloat16)
        queries = queries.reshape(REQUESTS, CANDS, HEADS, HEAD_DIM)
        partials = []
        for slice_pos in range(N_TM):
            live_len = (length_group - slice_pos * SLICE_LEN).astype(jnp.int32)
            partials.append(slice_partials(queries, keys_list[slice_pos], values_list[slice_pos], live_len))
        best_peak = partials[0][0]
        for part_here in partials[1:]:
            best_peak = jnp.maximum(best_peak, part_here[0])
        denom = jnp.zeros(best_peak.shape, jnp.float32)
        numer = jnp.zeros((REQUESTS, CANDS, HEADS, HEAD_DIM), jnp.float32)
        for part_here in partials:
            rescale = jnp.exp(part_here[0] - best_peak)
            denom = denom + rescale * part_here[1]
            numer = numer + jnp.transpose(rescale, (0, 2, 1))[..., None] * part_here[2]
        attended = (numer / jnp.transpose(denom, (0, 2, 1))[..., None]).reshape(REQUESTS * CANDS, EMBED).astype(jnp.bfloat16)
        return jnp.dot(attended, w_out, preferred_element_type=jnp.float32).astype(jnp.bfloat16)
    result = lax.map(one_group, (fetch_rows, tile_counts, hist_source, cand_source, lengths))
    return result.reshape(GROUPS * REQUESTS * CANDS, EMBED)
```

```python
import functools
import math

import jax
import jax.numpy as jnp
from jax import lax
from jax.experimental import pallas as pl
from jax.experimental.pallas import tpu as pltpu
from jax.sharding import PartitionSpec as P

HEADS = 4
TILE = 128
HEAD_ROWS = 48
PART_ROWS = 40
ROW_STEP = 2048
SUB = 256
GATHER_STEP = 256
VMEM_LIMIT = 58 << 20
NEG_FILL = -1e30

VMEM = pl.BlockSpec(memory_space=pltpu.VMEM)
SMEM = pl.BlockSpec(memory_space=pltpu.SMEM)


def owner_gather_kernel(chunk, asked, table, out, wide, rows_wide):
    devices, capacity = out.shape[0], asked.shape[0] // out.shape[0]
    step = 1024

    def widen(i, carry):
        rows = pl.ds(pl.multiple_of(i * step, step), step)
        wide[rows, :] = table[rows, :].astype(jnp.float32)
        return carry

    lax.fori_loop(0, table.shape[0] // step, widen, 0)

    def one_device(d, carry):
        base = d * capacity + chunk * TILE
        for j in range(TILE):
            rows_wide[j : j + 1, :] = wide[pl.ds(asked[base + j], 1), :]
        out[d] = rows_wide[...].astype(out.dtype)
        return carry

    lax.fori_loop(0, devices, one_device, 0)


def owner_gather(chunk, asked, table, devices):
    return pl.pallas_call(
        functools.partial(owner_gather_kernel, chunk),
        out_shape=jax.ShapeDtypeStruct((devices, TILE, table.shape[1]), table.dtype),
        in_specs=[SMEM, VMEM],
        out_specs=VMEM,
        scratch_shapes=[
            pltpu.VMEM(table.shape, jnp.float32),
            pltpu.VMEM((TILE, table.shape[1]), jnp.float32),
        ],
        compiler_params=pltpu.CompilerParams(vmem_limit_bytes=VMEM_LIMIT),
        cost_estimate=pl.CostEstimate(flops=0, bytes_accessed=40 << 20, transcendentals=0),
        name=f"owner_gather_{chunk}",
    )(asked, table)


def slot_gather_kernel(source, *refs):
    chunks, (out, wide, rows_wide) = refs[:-3], refs[-3:]
    per = chunks[0].shape[0]
    step = 1024

    for k, chunk in enumerate(chunks):

        def widen(i, carry, k=k, chunk=chunk):
            rows = pl.ds(pl.multiple_of(i * step, step), step)
            there = pl.ds(pl.multiple_of(k * per + i * step, step), step)
            wide[there, :] = chunk[rows, :].astype(jnp.float32)
            return carry

        lax.fori_loop(0, per // step, widen, 0)

    def group(i, carry):
        base = pl.multiple_of(i * GATHER_STEP, GATHER_STEP)
        for j in range(GATHER_STEP):
            rows_wide[j : j + 1, :] = wide[pl.ds(source[base + j], 1), :]
        out[pl.ds(base, GATHER_STEP), :] = rows_wide[...].astype(out.dtype)
        return carry

    lax.fori_loop(0, source.shape[0] // GATHER_STEP, group, 0)


def slot_gather(source, chunks):
    width = chunks[0].shape[1]
    return pl.pallas_call(
        slot_gather_kernel,
        out_shape=jax.ShapeDtypeStruct((source.shape[0], width), chunks[0].dtype),
        in_specs=[SMEM] + [VMEM] * len(chunks),
        out_specs=VMEM,
        scratch_shapes=[
            pltpu.VMEM((len(chunks) * chunks[0].shape[0], width), jnp.float32),
            pltpu.VMEM((GATHER_STEP, width), jnp.float32),
        ],
        compiler_params=pltpu.CompilerParams(vmem_limit_bytes=VMEM_LIMIT),
        name="slot_gather",
    )(source, *chunks)


def attention_kernel(
    slice_len, cand_block, live_ref, hist, queries, w_key, w_value, out, keys, values, qt, s_a, s_b
):
    f32, bf16 = jnp.float32, jnp.bfloat16
    requests = live_ref.shape[0]
    blocks = queries.shape[0] // cand_block // requests
    items = blocks * HEADS
    head_dim = keys.shape[1] // HEADS
    scale = 1.0 / math.sqrt(head_dim)
    to_exp2 = scale * math.log2(math.e)
    head_of = lax.broadcasted_iota(jnp.int32, (keys.shape[1], cand_block), 0) // head_dim
    lowest = jnp.full((8, cand_block), -jnp.inf, f32)
    steps = slice_len // ROW_STEP
    proj_step = 1024

    def one_request(r, carry):
        live = live_ref[r]
        for b in range(blocks):
            rows = pl.ds(pl.multiple_of((r * blocks + b) * cand_block, cand_block), cand_block)
            turned = queries[rows, :].astype(f32).T
            for h in range(HEADS):
                qt[b * HEADS + h] = jnp.where(head_of == h, turned, 0.0).astype(bf16)

        def project(i, c):
            rows = pl.ds(pl.multiple_of(i * proj_step, proj_step), proj_step)
            x = hist[pl.ds(pl.multiple_of(r * slice_len + i * proj_step, proj_step), proj_step), :]
            keys[rows, :] = jnp.dot(x, w_key[...], preferred_element_type=f32).astype(bf16)
            turned = lax.dot_general(
                w_value[...], x, (((0,), (1,)), ((), ())), preferred_element_type=f32
            )
            visible = lax.broadcasted_iota(jnp.int32, (1, proj_step), 1) + i * proj_step < live
            turned = jnp.where(visible, turned, 0.0).astype(bf16)
            first = lax.broadcasted_iota(jnp.int32, (16, proj_step), 0) == 0
            ones = jnp.where(first, jnp.where(visible, 1.0, 0.0), 0.0).astype(bf16)
            for h in range(HEADS):
                values[h, 0:head_dim, rows] = turned[h * head_dim : (h + 1) * head_dim]
                values[h, head_dim:HEAD_ROWS, rows] = ones
            return c

        lax.fori_loop(0, slice_len // proj_step, project, 0)

        def score(item, base, peak, scores):
            s = jnp.dot(keys[pl.ds(base, SUB), :], qt[item], preferred_element_type=f32)
            scores[pl.ds(base, SUB), :] = s
            return jnp.maximum(peak, jnp.max(s.reshape(SUB // 8, 8, cand_block), axis=0))

        def first_scores(i, peak):
            for j in range(ROW_STEP // SUB):
                peak = score(0, pl.multiple_of(i * ROW_STEP + j * SUB, SUB), peak, s_a)
            return peak

        def one_item(item, peak, scores, next_scores):
            top = jnp.max(peak, axis=0, keepdims=True)
            h = lax.rem(item, HEADS)
            following = jnp.minimum(item + 1, items - 1)

            def step(i, c):
                next_peak, total = c
                for j in range(ROW_STEP // SUB):
                    base = pl.multiple_of(i * ROW_STEP + j * SUB, SUB)
                    next_peak = score(following, base, next_peak, next_scores)
                    rows = pl.ds(base, SUB)
                    weights = jnp.exp2((scores[rows, :] - top) * to_exp2).astype(bf16)
                    total = total + jnp.dot(
                        values[h, :, rows], weights, preferred_element_type=f32
                    )
                return next_peak, total

            next_peak, total = lax.fori_loop(
                0, steps, step, (lowest, jnp.zeros((HEAD_ROWS, cand_block), f32))
            )
            shown = jnp.where(live > 0, top * scale, NEG_FILL)
            row = lax.broadcasted_iota(jnp.int32, (8, cand_block), 0)
            at = r * blocks + item // HEADS
            out[at, h, 0:head_dim, :] = total[0:head_dim]
            out[at, h, head_dim:PART_ROWS, :] = jnp.where(
                row == 1, shown, total[head_dim:PART_ROWS]
            )
            return next_peak

        def two_items(k, peak):
            peak = one_item(2 * k, peak, s_a, s_b)
            return one_item(2 * k + 1, peak, s_b, s_a)

        lax.fori_loop(0, items // 2, two_items, lax.fori_loop(0, steps, first_scores, lowest))
        return carry

    lax.fori_loop(0, requests, one_request, 0)


def attention(live, hist, queries, w_key, w_value, cand_block):
    requests = live.shape[0]
    slice_len = hist.shape[0] // requests
    width = hist.shape[1]
    blocks = queries.shape[0] // cand_block
    return pl.pallas_call(
        functools.partial(attention_kernel, slice_len, cand_block),
        out_shape=jax.ShapeDtypeStruct((blocks, HEADS, PART_ROWS, cand_block), jnp.float32),
        in_specs=[SMEM] + [VMEM] * 4,
        out_specs=VMEM,
        scratch_shapes=[
            pltpu.VMEM((slice_len, width), jnp.bfloat16),
            pltpu.VMEM((HEADS, HEAD_ROWS, slice_len), jnp.bfloat16),
            pltpu.VMEM((blocks // requests * HEADS, width, cand_block), jnp.bfloat16),
            pltpu.VMEM((slice_len, cand_block), jnp.float32),
            pltpu.VMEM((slice_len, cand_block), jnp.float32),
        ],
        compiler_params=pltpu.CompilerParams(vmem_limit_bytes=VMEM_LIMIT),
        name="attention",
    )(live, hist, queries, w_key, w_value)


def combine_kernel(parts, w_out, out):
    slices = parts.shape[0]
    head_dim = w_out.shape[0] // HEADS
    heads = []
    for h in range(HEADS):
        peaks = [parts[s, h, head_dim + 1 : head_dim + 2, :] for s in range(slices)]
        best = functools.reduce(jnp.maximum, peaks)
        denom = numer = 0.0
        for s in range(slices):
            rescale = jnp.exp(peaks[s] - best)
            denom = denom + rescale * parts[s, h, head_dim : head_dim + 1, :]
            numer = numer + rescale * parts[s, h, 0:head_dim, :]
        heads.append(numer / denom)
    attended = jnp.concatenate(heads, axis=0).T.astype(jnp.bfloat16)
    out[...] = jnp.dot(attended, w_out[...], preferred_element_type=jnp.float32).astype(out.dtype)


def combine(parts, w_out):
    return pl.pallas_call(
        combine_kernel,
        out_shape=jax.ShapeDtypeStruct((parts.shape[3], w_out.shape[1]), jnp.bfloat16),
        in_specs=[VMEM, VMEM],
        out_specs=VMEM,
        name="combine",
    )(parts, w_out)


def shards(
    table,
    fetch_rows,
    tile_counts,
    hist_source,
    cand_source,
    lengths,
    w_query,
    w_key,
    w_value,
    w_out,
):
    del tile_counts
    owners, capacity = fetch_rows.shape[2:]
    tiles = capacity // TILE
    requests, slice_len = hist_source.shape[2:]
    cand_dev = cand_source.shape[2]
    asked = lax.all_to_all(fetch_rows[0, 0], "tbl", split_axis=0, concat_axis=0, tiled=True)
    asked = asked.reshape(-1)
    chunks = []
    for chunk in range(tiles):
        looked = owner_gather(chunk, asked, table, owners)
        there = lax.all_to_all(looked, "tbl", split_axis=0, concat_axis=0, tiled=True)
        chunks.append(there.reshape(owners * TILE, table.shape[1]))

    def place(slot):
        tile = slot % capacity // TILE
        return tile * (owners * TILE) + slot // capacity * TILE + slot % TILE

    live = lengths[0] - lax.axis_index("tm") * slice_len
    source = hist_source[0, 0]
    position = jnp.arange(slice_len, dtype=jnp.int32)[None, :]
    source = jnp.where(position < live[:, None], source, source[:, :1]).reshape(-1)
    source = place(jnp.concatenate((cand_source[0, 0], source)))
    rows = slot_gather(source, chunks)
    own_cands, hist = rows[:cand_dev], rows[cand_dev:]
    cands = lax.all_gather(own_cands, "tm", axis=0, tiled=True)
    queries = jnp.dot(cands, w_query, preferred_element_type=jnp.float32).astype(jnp.bfloat16)
    parts = attention(live, hist, queries, w_key, w_value, cand_dev)
    parts = lax.all_to_all(parts, "tm", split_axis=0, concat_axis=0, tiled=True)
    return combine(parts, w_out)


def solution(mesh):
    return jax.shard_map(
        shards,
        mesh=mesh,
        in_specs=(
            P("tbl", None),
            P("tbl", "tm", None, None),
            P("tbl", "tm", None),
            P("tbl", "tm", None, None),
            P("tbl", "tm", None),
            P("tbl", None),
            P(),
            P(),
            P(),
            P(),
        ),
        out_specs=P(("tbl", "tm"), None),
        check_vma=False,
    )
```

```python
import functools
import math

import jax
import jax.numpy as jnp
from jax import lax
from jax.experimental import pallas as pl
from jax.experimental.pallas import tpu as pltpu
from jax.sharding import PartitionSpec as P

HEADS = 4
TILE = 128
CAND_DEV = 512
HEAD_ROWS = 48
PART_ROWS = 40
ROW_STEP = 2048
SUB = 256
GATHER_STEP = 256
VMEM_LIMIT = 58 << 20
NEG_FILL = -1e30

VMEM = pl.BlockSpec(memory_space=pltpu.VMEM)
SMEM = pl.BlockSpec(memory_space=pltpu.SMEM)
MESH = pl.DeviceIdType.MESH
STRIDE = 27


def fetch_kernel(
    devices,
    ids,
    table,
    out,
    wide,
    landing,
    asked,
    rows_wide,
    found,
    ids_send,
    ids_recv,
    row_send,
    row_recv,
    own_sem,
):
    me = lax.axis_index("tbl")
    capacity = found.shape[1]

    def forward(k):
        return lax.rem(me + k * STRIDE, devices)

    barrier = pltpu.get_barrier_semaphore()

    def greet(k, carry):
        pl.semaphore_signal(barrier, 1, device_id={"tbl": forward(k)}, device_id_type=MESH)
        return carry

    lax.fori_loop(1, devices, greet, 0)
    pl.semaphore_wait(barrier, devices - 1)

    def ids_copy(k):
        peer = forward(k)
        return pltpu.make_async_remote_copy(
            src_ref=ids.at[peer],
            dst_ref=landing.at[me],
            send_sem=ids_send.at[k],
            recv_sem=ids_recv.at[k],
            device_id={"tbl": peer},
            device_id_type=MESH,
        )

    def send_ids(k, carry):
        ids_copy(k).start()
        return carry

    lax.fori_loop(1, devices, send_ids, 0)
    landing[me] = ids[me]
    step = 1024

    def widen(i, carry):
        rows = pl.ds(pl.multiple_of(i * step, step), step)
        wide[rows, :] = table[rows, :].astype(jnp.float32)
        return carry

    lax.fori_loop(0, table.shape[0] // step, widen, 0)

    def wait_ids(k, carry):
        ids_copy(k).wait()
        return carry

    lax.fori_loop(1, devices, wait_ids, 0)
    listed = pltpu.make_async_copy(landing, asked, own_sem)
    listed.start()
    listed.wait()

    def look_up(k):
        peer = forward(k)

        def group(i, carry):
            for j in range(GATHER_STEP):
                row = asked[peer, i * (GATHER_STEP // TILE) + j // TILE, j % TILE]
                rows_wide[j : j + 1, :] = wide[pl.ds(row, 1), :]
            rows = pl.ds(pl.multiple_of(i * GATHER_STEP, GATHER_STEP), GATHER_STEP)
            found[k, rows, :] = rows_wide[...].astype(found.dtype)
            return carry

        lax.fori_loop(0, capacity // GATHER_STEP, group, 0)

    def row_copy(k):
        return pltpu.make_async_remote_copy(
            src_ref=found.at[k],
            dst_ref=out.at[me],
            send_sem=row_send.at[k],
            recv_sem=row_recv.at[k],
            device_id={"tbl": forward(k)},
            device_id_type=MESH,
        )

    def send_rows(k, carry):
        look_up(k)
        row_copy(k).start()
        return carry

    lax.fori_loop(1, devices, send_rows, 0)
    look_up(0)
    own = pltpu.make_async_copy(found.at[0], out.at[me], own_sem)
    own.start()

    def wait_rows(k, carry):
        row_copy(k).wait()
        return carry

    lax.fori_loop(1, devices, wait_rows, 0)
    own.wait()


def fetch(ids, table):
    devices, capacity = ids.shape
    width = table.shape[1]
    tiles = capacity // TILE
    return pl.pallas_call(
        functools.partial(fetch_kernel, devices),
        out_shape=jax.ShapeDtypeStruct((devices, capacity, width), table.dtype),
        in_specs=[VMEM, VMEM],
        out_specs=pl.BlockSpec(memory_space=pl.ANY),
        scratch_shapes=[
            pltpu.VMEM(table.shape, jnp.float32),
            pltpu.VMEM((devices, tiles, TILE), jnp.int32),
            pltpu.SMEM((devices, tiles, TILE), jnp.int32),
            pltpu.VMEM((GATHER_STEP, width), jnp.float32),
            pltpu.VMEM((devices, capacity, width), table.dtype),
        ]
        + [pltpu.SemaphoreType.DMA((devices,))] * 4
        + [pltpu.SemaphoreType.DMA],
        compiler_params=pltpu.CompilerParams(
            collective_id=1, has_side_effects=True, vmem_limit_bytes=VMEM_LIMIT
        ),
        name="fetch",
    )(ids.reshape(devices, tiles, TILE), table)


def attend_kernel(
    live_ref,
    source,
    fetched,
    w_query,
    w_key,
    w_value,
    w_out,
    out,
    wide,
    scores_b,
    rows_wide,
    cands,
    hist,
    keys,
    values,
    qt,
    parts,
    arrived,
    cand_send,
    cand_recv,
    part_send,
    part_recv,
):
    f32, bf16 = jnp.float32, jnp.bfloat16
    slices, cand_block = cands.shape[:2]
    requests = live_ref.shape[0]
    width = keys.shape[1]
    slice_len = keys.shape[0]
    blocks = slices // requests
    items = blocks * HEADS
    head_dim = width // HEADS
    scale = 1.0 / math.sqrt(head_dim)
    to_exp2 = scale * math.log2(math.e)
    me = lax.axis_index("tm")

    barrier = pltpu.get_barrier_semaphore()
    for off in range(1, slices):
        pl.semaphore_signal(
            barrier, 1, device_id={"tm": lax.rem(me + off, slices)}, device_id_type=MESH
        )
    pl.semaphore_wait(barrier, slices - 1)

    step = 1024

    def widen(i, carry):
        rows = pl.ds(pl.multiple_of(i * step, step), step)
        wide[rows, :] = fetched[rows, :].astype(f32)
        return carry

    lax.fori_loop(0, fetched.shape[0] // step, widen, 0)

    def gather(first):
        for j in range(GATHER_STEP):
            rows_wide[j : j + 1, :] = wide[pl.ds(source[first + j], 1), :]
        return rows_wide[...].astype(bf16)

    def cand_group(i, carry):
        base = pl.multiple_of(i * GATHER_STEP, GATHER_STEP)
        cands[me, pl.ds(base, GATHER_STEP), :] = gather(base)
        return carry

    lax.fori_loop(0, cand_block // GATHER_STEP, cand_group, 0)

    def cand_copy(off):
        return pltpu.make_async_remote_copy(
            src_ref=cands.at[me],
            dst_ref=cands.at[me],
            send_sem=cand_send.at[off],
            recv_sem=cand_recv.at[off],
            device_id={"tm": lax.rem(me + off, slices)},
            device_id_type=MESH,
        )

    for off in range(1, slices):
        cand_copy(off).start()

    def hist_group(i, carry):
        base = pl.multiple_of(i * GATHER_STEP, GATHER_STEP)
        hist[pl.ds(base, GATHER_STEP), :] = gather(cand_block + base)
        return carry

    lax.fori_loop(0, requests * slice_len // GATHER_STEP, hist_group, 0)
    for off in range(1, slices):
        cand_copy(off).wait()

    def part_copy(off, h):
        there = lax.rem(me + off, slices)
        return pltpu.make_async_remote_copy(
            src_ref=parts.at[there, h],
            dst_ref=arrived.at[me, h],
            send_sem=part_send.at[off, h],
            recv_sem=part_recv.at[off, h],
            device_id={"tm": there},
            device_id_type=MESH,
        )

    head_of = lax.broadcasted_iota(jnp.int32, (width, cand_block), 0) // head_dim
    lowest = jnp.full((8, cand_block), -jnp.inf, f32)
    steps = slice_len // ROW_STEP
    lanes = cand_block // TILE

    def put_a(base, s):
        for c in range(lanes):
            wide[pl.ds(c * slice_len + base, SUB), :] = s[:, c * TILE : (c + 1) * TILE]

    def get_a(base):
        return jnp.concatenate(
            [wide[pl.ds(c * slice_len + base, SUB), :] for c in range(lanes)], axis=1
        )

    def put_b(base, s):
        scores_b[pl.ds(base, SUB), :] = s

    def get_b(base):
        return scores_b[pl.ds(base, SUB), :]

    def one_request(turn, carry):
        r = lax.rem(me // blocks + 1 + turn, requests)
        live = live_ref[r]

        def block_of(j):
            return r * blocks + lax.rem(me + 1 + j, blocks)

        for b in range(blocks):
            query = jnp.dot(cands[block_of(b)], w_query[...], preferred_element_type=f32)
            turned = query.astype(bf16).astype(f32).T
            for h in range(HEADS):
                qt[b * HEADS + h] = jnp.where(head_of == h, turned, 0.0).astype(bf16)

        def project(i, c):
            rows = pl.ds(pl.multiple_of(i * step, step), step)
            x = hist[pl.ds(pl.multiple_of(r * slice_len + i * step, step), step), :]
            keys[rows, :] = jnp.dot(x, w_key[...], preferred_element_type=f32).astype(bf16)
            turned = lax.dot_general(
                w_value[...], x, (((0,), (1,)), ((), ())), preferred_element_type=f32
            )
            visible = lax.broadcasted_iota(jnp.int32, (1, step), 1) + i * step < live
            turned = jnp.where(visible, turned, 0.0).astype(bf16)
            first = lax.broadcasted_iota(jnp.int32, (16, step), 0) == 0
            ones = jnp.where(first, jnp.where(visible, 1.0, 0.0), 0.0).astype(bf16)
            for h in range(HEADS):
                values[h, 0:head_dim, rows] = turned[h * head_dim : (h + 1) * head_dim]
                values[h, head_dim:HEAD_ROWS, rows] = ones
            return c

        lax.fori_loop(0, slice_len // step, project, 0)

        def score(item, base, peak, put):
            s = jnp.dot(keys[pl.ds(base, SUB), :], qt[item], preferred_element_type=f32)
            put(base, s)
            return jnp.maximum(peak, jnp.max(s.reshape(SUB // 8, 8, cand_block), axis=0))

        def first_scores(i, peak):
            for j in range(ROW_STEP // SUB):
                peak = score(0, pl.multiple_of(i * ROW_STEP + j * SUB, SUB), peak, put_a)
            return peak

        def one_item(item, peak, get, put_next):
            top = jnp.max(peak, axis=0, keepdims=True)
            h = lax.rem(item, HEADS)
            following = jnp.minimum(item + 1, items - 1)

            def attend_step(i, c):
                next_peak, total = c
                for j in range(ROW_STEP // SUB):
                    base = pl.multiple_of(i * ROW_STEP + j * SUB, SUB)
                    next_peak = score(following, base, next_peak, put_next)
                    weights = jnp.exp2((get(base) - top) * to_exp2).astype(bf16)
                    total = total + jnp.dot(
                        values[h, :, pl.ds(base, SUB)], weights, preferred_element_type=f32
                    )
                return next_peak, total

            next_peak, total = lax.fori_loop(
                0, steps, attend_step, (lowest, jnp.zeros((HEAD_ROWS, cand_block), f32))
            )
            shown = jnp.where(live > 0, top * scale, NEG_FILL)
            row = lax.broadcasted_iota(jnp.int32, (8, cand_block), 0)
            tail = jnp.where(row == 1, shown, total[head_dim:PART_ROWS])
            there = block_of(item // HEADS)

            @pl.when(there != me)
            def _():
                parts[there, h, 0:head_dim, :] = total[0:head_dim]
                parts[there, h, head_dim:PART_ROWS, :] = tail
                part_copy(lax.rem(there - me + slices, slices), h).start()

            @pl.when(there == me)
            def _():
                arrived[me, h, 0:head_dim, :] = total[0:head_dim]
                arrived[me, h, head_dim:PART_ROWS, :] = tail

            return next_peak

        def two_items(k, peak):
            peak = one_item(2 * k, peak, get_a, put_b)
            return one_item(2 * k + 1, peak, get_b, put_a)

        lax.fori_loop(0, items // 2, two_items, lax.fori_loop(0, steps, first_scores, lowest))
        return carry

    lax.fori_loop(0, requests, one_request, 0)
    for off in range(1, slices):
        for h in range(HEADS):
            part_copy(off, h).wait()

    heads = []
    for h in range(HEADS):
        peaks = [arrived[s, h, head_dim + 1 : head_dim + 2, :] for s in range(slices)]
        best = functools.reduce(jnp.maximum, peaks)
        denom = numer = 0.0
        for s in range(slices):
            rescale = jnp.exp(peaks[s] - best)
            denom = denom + rescale * arrived[s, h, head_dim : head_dim + 1, :]
            numer = numer + rescale * arrived[s, h, 0:head_dim, :]
        heads.append(numer / denom)
    attended = jnp.concatenate(heads, axis=0).T.astype(bf16)
    out[...] = jnp.dot(attended, w_out[...], preferred_element_type=f32).astype(out.dtype)


def attend(live, source, fetched, w_query, w_key, w_value, w_out, slices):
    requests = live.shape[0]
    width = fetched.shape[1]
    cand_block = CAND_DEV
    slice_len = (source.shape[0] - cand_block) // requests
    bf16, f32 = jnp.bfloat16, jnp.float32
    part = (slices, HEADS, PART_ROWS, cand_block)
    return pl.pallas_call(
        attend_kernel,
        out_shape=jax.ShapeDtypeStruct((cand_block, w_out.shape[1]), bf16),
        in_specs=[SMEM, SMEM] + [VMEM] * 5,
        out_specs=VMEM,
        scratch_shapes=[
            pltpu.VMEM(fetched.shape, f32),
            pltpu.VMEM((slice_len, cand_block), f32),
            pltpu.VMEM((GATHER_STEP, width), f32),
            pltpu.VMEM((slices, cand_block, width), bf16),
            pltpu.VMEM((requests * slice_len, width), bf16),
            pltpu.VMEM((slice_len, width), bf16),
            pltpu.VMEM((HEADS, HEAD_ROWS, slice_len), bf16),
            pltpu.VMEM((slices // requests * HEADS, width, cand_block), bf16),
            pltpu.VMEM(part, f32),
            pltpu.VMEM(part, f32),
            pltpu.SemaphoreType.DMA((slices,)),
            pltpu.SemaphoreType.DMA((slices,)),
            pltpu.SemaphoreType.DMA((slices, HEADS)),
            pltpu.SemaphoreType.DMA((slices, HEADS)),
        ],
        compiler_params=pltpu.CompilerParams(
            collective_id=2, has_side_effects=True, vmem_limit_bytes=VMEM_LIMIT
        ),
        name="attend",
    )(live, source, fetched, w_query, w_key, w_value, w_out)


def shards(
    table,
    fetch_rows,
    tile_counts,
    hist_source,
    cand_source,
    lengths,
    w_query,
    w_key,
    w_value,
    w_out,
):
    del tile_counts
    requests, slice_len = hist_source.shape[2:]
    fetched = fetch(fetch_rows[0, 0], table).reshape(-1, table.shape[1])
    live = lengths[0] - lax.axis_index("tm") * slice_len
    source = hist_source[0, 0]
    position = jnp.arange(slice_len, dtype=jnp.int32)[None, :]
    source = jnp.where(position < live[:, None], source, source[:, :1]).reshape(-1)
    source = jnp.concatenate((cand_source[0, 0], source))
    slices = lax.axis_size("tm")
    return attend(live, source, fetched, w_query, w_key, w_value, w_out, slices)


def solution(mesh):
    return jax.shard_map(
        shards,
        mesh=mesh,
        in_specs=(
            P("tbl", None),
            P("tbl", "tm", None, None),
            P("tbl", "tm", None),
            P("tbl", "tm", None, None),
            P("tbl", "tm", None),
            P("tbl", None),
            P(),
            P(),
            P(),
            P(),
        ),
        out_specs=P(("tbl", "tm"), None),
        check_vma=False,
    )
```

```python
import functools
import math

import jax
import jax.numpy as jnp
from jax import lax
from jax.experimental import pallas as pl
from jax.experimental.pallas import tpu as pltpu
from jax.sharding import PartitionSpec as P

HEADS = 4
TILE = 128
HEAD_ROWS = 48
PART_ROWS = 40
ROW_STEP = 2048
SUB = 256
GATHER_STEP = 256
TABLE_PIECES = 8
STRIDE = 27
VMEM_LIMIT = 60 << 20
NEG_FILL = -1e30

VMEM = pl.BlockSpec(memory_space=pltpu.VMEM)
SMEM = pl.BlockSpec(memory_space=pltpu.SMEM)
ANY = pl.BlockSpec(memory_space=pl.ANY)
MESH = pl.DeviceIdType.MESH


def kernel(
    devices,
    slices,
    lengths,
    hist_source,
    cand_source,
    ids,
    table,
    w_query,
    w_key,
    w_value,
    w_out,
    out,
    wide,
    found,
    landing,
    scores_b,
    ids_landing,
    asked,
    rows_wide,
    cands,
    values,
    qt,
    parts,
    arrived,
    table_sem,
    asked_sem,
    ids_send,
    ids_recv,
    row_send,
    row_recv,
    cand_send,
    cand_recv,
    part_send,
    part_recv,
):
    f32, bf16 = jnp.float32, jnp.bfloat16
    me, my_slice = lax.axis_index("tbl"), lax.axis_index("tm")
    capacity, width = found.shape[1:]
    cand_block = cands.shape[1]
    requests, slice_len = hist_source.shape
    blocks = slices // requests
    items = blocks * HEADS
    head_dim = width // HEADS
    scale = 1.0 / math.sqrt(head_dim)
    to_exp2 = scale * math.log2(math.e)

    def forward(k):
        return lax.rem(me + k * STRIDE, devices)

    def backward(k):
        return lax.rem(me + k * (devices - STRIDE), devices)

    def other_slice(off):
        return lax.rem(my_slice + off, slices)

    per_piece = devices // TABLE_PIECES

    def table_copy(p):
        part = pl.ds(p * per_piece, per_piece)
        return pltpu.make_async_copy(table.at[part], found.at[part], table_sem.at[p])

    for p in range(TABLE_PIECES):
        table_copy(p).start()

    barrier = pltpu.get_barrier_semaphore()

    def greet(k, carry):
        pl.semaphore_signal(barrier, 1, device_id={"tbl": forward(k)}, device_id_type=MESH)
        return carry

    lax.fori_loop(1, devices, greet, 0)
    for off in range(1, slices):
        pl.semaphore_signal(barrier, 1, device_id={"tm": other_slice(off)}, device_id_type=MESH)
    pl.semaphore_wait(barrier, devices - 1 + slices - 1)

    def ids_copy(k):
        peer = forward(k)
        return pltpu.make_async_remote_copy(
            src_ref=ids.at[peer],
            dst_ref=ids_landing.at[me],
            send_sem=ids_send.at[k],
            recv_sem=ids_recv.at[k],
            device_id={"tbl": peer},
            device_id_type=MESH,
        )

    def send_ids(k, carry):
        ids_copy(k).start()
        return carry

    lax.fori_loop(1, devices, send_ids, 0)
    ids_landing[me] = ids[me]

    def widen(buffer, d):
        rows = pl.ds(pl.multiple_of(d * capacity, capacity), capacity)
        wide[rows, :] = buffer[d].astype(f32)

    for p in range(TABLE_PIECES):
        table_copy(p).wait()

        def widen_table(i, carry, p=p):
            widen(found, p * per_piece + i)
            return carry

        lax.fori_loop(0, per_piece, widen_table, 0)

    def wait_ids(k, carry):
        ids_copy(k).wait()
        return carry

    lax.fori_loop(1, devices, wait_ids, 0)
    listed = pltpu.make_async_copy(ids_landing, asked, asked_sem)
    listed.start()
    listed.wait()

    def look_up(k):
        peer = forward(k)

        def group(i, carry):
            for j in range(GATHER_STEP):
                row = asked[peer, i * (GATHER_STEP // TILE) + j // TILE, j % TILE]
                rows_wide[j : j + 1, :] = wide[pl.ds(row, 1), :]
            rows = pl.ds(pl.multiple_of(i * GATHER_STEP, GATHER_STEP), GATHER_STEP)
            found[k, rows, :] = rows_wide[...].astype(bf16)
            return carry

        lax.fori_loop(0, capacity // GATHER_STEP, group, 0)

    def row_copy(k):
        return pltpu.make_async_remote_copy(
            src_ref=found.at[k],
            dst_ref=landing.at[me],
            send_sem=row_send.at[k],
            recv_sem=row_recv.at[k],
            device_id={"tbl": forward(k)},
            device_id_type=MESH,
        )

    def send_rows(k, carry):
        look_up(k)
        row_copy(k).start()
        return carry

    lax.fori_loop(1, devices, send_rows, 0)
    look_up(0)
    own_rows = pl.ds(pl.multiple_of(me * capacity, capacity), capacity)
    wide[own_rows, :] = found[0].astype(f32)

    def take_rows(k, carry):
        row_copy(k).wait()
        widen(landing, backward(k))
        return carry

    lax.fori_loop(1, devices, take_rows, 0)

    def gather(pick):
        for j in range(GATHER_STEP):
            rows_wide[j : j + 1, :] = wide[pl.ds(pick(j), 1), :]
        return rows_wide[...].astype(bf16)

    def cand_group(i, carry):
        base = pl.multiple_of(i * GATHER_STEP, GATHER_STEP)
        cands[my_slice, pl.ds(base, GATHER_STEP), :] = gather(lambda j: cand_source[base + j])
        return carry

    lax.fori_loop(0, cand_block // GATHER_STEP, cand_group, 0)

    def cand_copy(off):
        return pltpu.make_async_remote_copy(
            src_ref=cands.at[my_slice],
            dst_ref=cands.at[my_slice],
            send_sem=cand_send.at[off],
            recv_sem=cand_recv.at[off],
            device_id={"tm": other_slice(off)},
            device_id_type=MESH,
        )

    for off in range(1, slices):
        cand_copy(off).start()

    pieces = slice_len // capacity
    halves = capacity // GATHER_STEP

    def hist_group(n, carry):
        r = n // (pieces * halves)
        base = pl.multiple_of(n % (pieces * halves) * GATHER_STEP, GATHER_STEP)
        rows = pl.ds(pl.multiple_of(n % halves * GATHER_STEP, GATHER_STEP), GATHER_STEP)
        found[n // halves, rows, :] = gather(lambda j: hist_source[r, base + j])
        return carry

    lax.fori_loop(0, requests * pieces * halves, hist_group, 0)
    for off in range(1, slices):
        cand_copy(off).wait()

    def part_copy(off, h):
        there = other_slice(off)
        return pltpu.make_async_remote_copy(
            src_ref=parts.at[there, h],
            dst_ref=arrived.at[my_slice, h],
            send_sem=part_send.at[off, h],
            recv_sem=part_recv.at[off, h],
            device_id={"tm": there},
            device_id_type=MESH,
        )

    head_of = lax.broadcasted_iota(jnp.int32, (width, cand_block), 0) // head_dim
    lowest = jnp.full((8, cand_block), -jnp.inf, f32)
    steps = slice_len // ROW_STEP
    lanes = cand_block // TILE
    subs = capacity // SUB

    def put_a(base, s):
        for c in range(lanes):
            wide[pl.ds(c * slice_len + base, SUB), :] = s[:, c * TILE : (c + 1) * TILE]

    def get_a(base):
        return jnp.concatenate(
            [wide[pl.ds(c * slice_len + base, SUB), :] for c in range(lanes)], axis=1
        )

    def put_b(base, s):
        scores_b[pl.ds(base, SUB), :] = s

    def get_b(base):
        return scores_b[pl.ds(base, SUB), :]

    def one_request(turn, carry):
        r = lax.rem(my_slice // blocks + 1 + turn, requests)
        live = lengths[r] - my_slice * slice_len

        def block_of(j):
            return r * blocks + lax.rem(my_slice + 1 + j, blocks)

        for b in range(blocks):
            query = jnp.dot(cands[block_of(b)], w_query[...], preferred_element_type=f32)
            turned = query.astype(bf16).astype(f32).T
            for h in range(HEADS):
                qt[b * HEADS + h] = jnp.where(head_of == h, turned, 0.0).astype(bf16)

        first_key = jnp.dot(found[r * pieces, 0:16, :], w_key[...], preferred_element_type=f32)[0:1]

        def project(i, c):
            rows = pl.ds(pl.multiple_of(i * capacity, capacity), capacity)
            x = found[r * pieces + i]
            key = jnp.dot(x, w_key[...], preferred_element_type=f32)
            down = lax.broadcasted_iota(jnp.int32, (capacity, width), 0) + i * capacity < live
            landing[i] = jnp.where(down, key, first_key).astype(bf16)
            turned = lax.dot_general(
                w_value[...], x, (((0,), (1,)), ((), ())), preferred_element_type=f32
            )
            visible = lax.broadcasted_iota(jnp.int32, (1, capacity), 1) + i * capacity < live
            turned = jnp.where(visible, turned, 0.0).astype(bf16)
            first = lax.broadcasted_iota(jnp.int32, (16, capacity), 0) == 0
            ones = jnp.where(first, jnp.where(visible, 1.0, 0.0), 0.0).astype(bf16)
            for h in range(HEADS):
                values[h, 0:head_dim, rows] = turned[h * head_dim : (h + 1) * head_dim]
                values[h, head_dim:HEAD_ROWS, rows] = ones
            return c

        lax.fori_loop(0, pieces, project, 0)

        def score(item, i, j, peak, put):
            keys = landing[i * (ROW_STEP // capacity) + j // subs, pl.ds(j % subs * SUB, SUB), :]
            s = jnp.dot(keys, qt[item], preferred_element_type=f32)
            put(pl.multiple_of(i * ROW_STEP + j * SUB, SUB), s)
            return jnp.maximum(peak, jnp.max(s.reshape(SUB // 8, 8, cand_block), axis=0))

        def first_scores(i, peak):
            for j in range(ROW_STEP // SUB):
                peak = score(0, i, j, peak, put_a)
            return peak

        def one_item(item, peak, get, put_next):
            top = jnp.max(peak, axis=0, keepdims=True)
            h = lax.rem(item, HEADS)
            following = jnp.minimum(item + 1, items - 1)

            def attend_step(i, c):
                next_peak, total = c
                for j in range(ROW_STEP // SUB):
                    base = pl.multiple_of(i * ROW_STEP + j * SUB, SUB)
                    next_peak = score(following, i, j, next_peak, put_next)
                    weights = jnp.exp2((get(base) - top) * to_exp2).astype(bf16)
                    total = total + jnp.dot(
                        values[h, :, pl.ds(base, SUB)], weights, preferred_element_type=f32
                    )
                return next_peak, total

            next_peak, total = lax.fori_loop(
                0, steps, attend_step, (lowest, jnp.zeros((HEAD_ROWS, cand_block), f32))
            )
            shown = jnp.where(live > 0, top * scale, NEG_FILL)
            row = lax.broadcasted_iota(jnp.int32, (8, cand_block), 0)
            tail = jnp.where(row == 1, shown, total[head_dim:PART_ROWS])
            there = block_of(item // HEADS)

            @pl.when(there != my_slice)
            def _():
                parts[there, h, 0:head_dim, :] = total[0:head_dim]
                parts[there, h, head_dim:PART_ROWS, :] = tail
                part_copy(lax.rem(there - my_slice + slices, slices), h).start()

            @pl.when(there == my_slice)
            def _():
                arrived[my_slice, h, 0:head_dim, :] = total[0:head_dim]
                arrived[my_slice, h, head_dim:PART_ROWS, :] = tail

            return next_peak

        def two_items(k, peak):
            peak = one_item(2 * k, peak, get_a, put_b)
            return one_item(2 * k + 1, peak, get_b, put_a)

        lax.fori_loop(0, items // 2, two_items, lax.fori_loop(0, steps, first_scores, lowest))
        return carry

    lax.fori_loop(0, requests, one_request, 0)
    for off in range(1, slices):
        for h in range(HEADS):
            part_copy(off, h).wait()

    heads = []
    for h in range(HEADS):
        peaks = [arrived[s, h, head_dim + 1 : head_dim + 2, :] for s in range(slices)]
        best = functools.reduce(jnp.maximum, peaks)
        denom = numer = 0.0
        for s in range(slices):
            rescale = jnp.exp(peaks[s] - best)
            denom = denom + rescale * arrived[s, h, head_dim : head_dim + 1, :]
            numer = numer + rescale * arrived[s, h, 0:head_dim, :]
        heads.append(numer / denom)
    attended = jnp.concatenate(heads, axis=0).T.astype(bf16)
    out[...] = jnp.dot(attended, w_out[...], preferred_element_type=f32).astype(out.dtype)


def shards(
    table,
    fetch_rows,
    tile_counts,
    hist_source,
    cand_source,
    lengths,
    w_query,
    w_key,
    w_value,
    w_out,
):
    del tile_counts
    devices, capacity = fetch_rows.shape[2:]
    slice_len = hist_source.shape[3]
    cand_block = cand_source.shape[2]
    width = table.shape[1]
    slices, tiles = lax.axis_size("tm"), capacity // TILE
    blocks = slices // hist_source.shape[2]
    f32, bf16 = jnp.float32, jnp.bfloat16
    rows = (devices, capacity, width)
    part = (slices, HEADS, PART_ROWS, cand_block)
    dma = pltpu.SemaphoreType.DMA
    return pl.pallas_call(
        functools.partial(kernel, devices, slices),
        out_shape=jax.ShapeDtypeStruct((cand_block, w_out.shape[1]), bf16),
        in_specs=[SMEM] * 3 + [VMEM, ANY] + [VMEM] * 4,
        out_specs=VMEM,
        scratch_shapes=[
            pltpu.VMEM(table.shape, f32),
            pltpu.VMEM(rows, bf16),
            pltpu.VMEM(rows, bf16),
            pltpu.VMEM((slice_len, cand_block), f32),
            pltpu.VMEM((devices, tiles, TILE), jnp.int32),
            pltpu.SMEM((devices, tiles, TILE), jnp.int32),
            pltpu.VMEM((GATHER_STEP, width), f32),
            pltpu.VMEM((slices, cand_block, width), bf16),
            pltpu.VMEM((HEADS, HEAD_ROWS, slice_len), bf16),
            pltpu.VMEM((blocks * HEADS, width, cand_block), bf16),
            pltpu.VMEM(part, f32),
            pltpu.VMEM(part, f32),
            dma((TABLE_PIECES,)),
            dma,
            dma((devices,)),
            dma((devices,)),
            dma((devices,)),
            dma((devices,)),
            dma((slices,)),
            dma((slices,)),
            dma((slices, HEADS)),
            dma((slices, HEADS)),
        ],
        compiler_params=pltpu.CompilerParams(
            collective_id=1, has_side_effects=True, vmem_limit_bytes=VMEM_LIMIT
        ),
        name="attend",
    )(
        lengths[0],
        hist_source[0, 0],
        cand_source[0, 0],
        fetch_rows.reshape(devices, tiles, TILE),
        table.reshape(rows),
        w_query,
        w_key,
        w_value,
        w_out,
    )


def solution(mesh):
    return jax.shard_map(
        shards,
        mesh=mesh,
        in_specs=(
            P("tbl", None),
            P("tbl", "tm", None, None),
            P("tbl", "tm", None),
            P("tbl", "tm", None, None),
            P("tbl", "tm", None),
            P("tbl", None),
            P(),
            P(),
            P(),
            P(),
        ),
        out_specs=P(("tbl", "tm"), None),
        check_vma=False,
    )
```

```python
import functools
import math

import jax
import jax.numpy as jnp
from jax import lax
from jax.experimental import pallas as pl
from jax.experimental.pallas import tpu as pltpu
from jax.sharding import PartitionSpec as P

HEADS = 4
TILE = 128
HEAD_ROWS = 48
PART_ROWS = 40
ROW_STEP = 2048
SUB = 256
GATHER_STEP = 256
TABLE_PIECES = 8
STRIDE = 27
VMEM_LIMIT = 62 << 20
NEG_FILL = -1e30

VMEM = pl.BlockSpec(memory_space=pltpu.VMEM)
SMEM = pl.BlockSpec(memory_space=pltpu.SMEM)
ANY = pl.BlockSpec(memory_space=pl.ANY)
MESH = pl.DeviceIdType.MESH


def kernel(
    devices,
    slices,
    lengths,
    hist_source,
    cand_source,
    ids,
    table,
    w_query,
    w_key,
    w_value,
    w_out,
    out,
    wide,
    found,
    landing,
    scores,
    ids_landing,
    asked,
    rows_wide,
    cands,
    values,
    qt,
    parts,
    arrived,
    table_sem,
    asked_sem,
    ids_send,
    ids_recv,
    row_send,
    row_recv,
    cand_send,
    cand_recv,
    part_send,
    part_recv,
):
    f32, bf16 = jnp.float32, jnp.bfloat16
    me, my_slice = lax.axis_index("tbl"), lax.axis_index("tm")
    capacity, width = found.shape[1:]
    cand_block = cands.shape[1]
    requests, slice_len = lengths.shape[0], hist_source.size // lengths.shape[0]
    blocks = slices // requests
    items = blocks * HEADS
    head_dim = width // HEADS
    scale = 1.0 / math.sqrt(head_dim)
    to_exp2 = scale * math.log2(math.e)

    def forward(k):
        return lax.rem(me + k * STRIDE, devices)

    def backward(k):
        return lax.rem(me + k * (devices - STRIDE), devices)

    def other_slice(off):
        return lax.rem(my_slice + off, slices)

    per_piece = devices // TABLE_PIECES

    def table_copy(p):
        part = pl.ds(p * per_piece, per_piece)
        return pltpu.make_async_copy(table.at[part], found.at[part], table_sem.at[p])

    for p in range(TABLE_PIECES):
        table_copy(p).start()

    barrier = pltpu.get_barrier_semaphore()

    def greet(k, carry):
        pl.semaphore_signal(barrier, 1, device_id={"tbl": forward(k)}, device_id_type=MESH)
        return carry

    lax.fori_loop(1, devices, greet, 0)
    for off in range(1, slices):
        pl.semaphore_signal(barrier, 1, device_id={"tm": other_slice(off)}, device_id_type=MESH)
    pl.semaphore_wait(barrier, devices - 1 + slices - 1)

    def ids_copy(k):
        peer = forward(k)
        return pltpu.make_async_remote_copy(
            src_ref=ids.at[peer],
            dst_ref=ids_landing.at[me],
            send_sem=ids_send.at[k],
            recv_sem=ids_recv.at[k],
            device_id={"tbl": peer},
            device_id_type=MESH,
        )

    def send_ids(k, carry):
        ids_copy(k).start()
        return carry

    lax.fori_loop(1, devices, send_ids, 0)
    ids_landing[me] = ids[me]

    def widen(buffer, d):
        rows = pl.ds(pl.multiple_of(d * capacity, capacity), capacity)
        wide[rows, :] = buffer[d].astype(f32)

    for p in range(TABLE_PIECES):
        table_copy(p).wait()

        def widen_table(i, carry, p=p):
            widen(found, p * per_piece + i)
            return carry

        lax.fori_loop(0, per_piece, widen_table, 0)

    def wait_ids(k, carry):
        ids_copy(k).wait()
        return carry

    lax.fori_loop(1, devices, wait_ids, 0)
    listed = pltpu.make_async_copy(ids_landing, asked, asked_sem)
    listed.start()
    listed.wait()

    def look_up(k):
        peer = forward(k)

        def group(i, carry):
            for j in range(GATHER_STEP):
                row = asked[peer, i * (GATHER_STEP // TILE) + j // TILE, j % TILE]
                rows_wide[j : j + 1, :] = wide[pl.ds(row, 1), :]
            rows = pl.ds(pl.multiple_of(i * GATHER_STEP, GATHER_STEP), GATHER_STEP)
            found[k, rows, :] = rows_wide[...].astype(bf16)
            return carry

        lax.fori_loop(0, capacity // GATHER_STEP, group, 0)

    def row_copy(k):
        return pltpu.make_async_remote_copy(
            src_ref=found.at[k],
            dst_ref=landing.at[me],
            send_sem=row_send.at[k],
            recv_sem=row_recv.at[k],
            device_id={"tbl": forward(k)},
            device_id_type=MESH,
        )

    def send_rows(k, carry):
        look_up(k)
        row_copy(k).start()
        return carry

    lax.fori_loop(1, devices, send_rows, 0)
    look_up(0)
    own_rows = pl.ds(pl.multiple_of(me * capacity, capacity), capacity)
    wide[own_rows, :] = found[0].astype(f32)

    def take_rows(k, carry):
        row_copy(k).wait()
        widen(landing, backward(k))
        return carry

    lax.fori_loop(1, devices, take_rows, 0)

    def gather(pick):
        for j in range(GATHER_STEP):
            rows_wide[j : j + 1, :] = wide[pl.ds(pick(j), 1), :]
        return rows_wide[...].astype(bf16)

    def cand_group(i, carry):
        base = pl.multiple_of(i * GATHER_STEP, GATHER_STEP)
        cands[my_slice, pl.ds(base, GATHER_STEP), :] = gather(lambda j: cand_source[base + j])
        return carry

    lax.fori_loop(0, cand_block // GATHER_STEP, cand_group, 0)

    def cand_copy(off):
        return pltpu.make_async_remote_copy(
            src_ref=cands.at[my_slice],
            dst_ref=cands.at[my_slice],
            send_sem=cand_send.at[off],
            recv_sem=cand_recv.at[off],
            device_id={"tm": other_slice(off)},
            device_id_type=MESH,
        )

    for off in range(1, slices):
        cand_copy(off).start()

    pieces = slice_len // capacity
    halves = capacity // GATHER_STEP
    order = [lax.rem(my_slice // blocks + 1 + turn, requests) for turn in range(requests)]

    def hist_piece(r, i):
        piece = r * pieces + i
        for half in range(halves):
            first = (piece * halves + half) * (GATHER_STEP // TILE)
            found[piece, half * GATHER_STEP : (half + 1) * GATHER_STEP, :] = gather(
                lambda j: hist_source[first + j // TILE, j % TILE]
            )

    def first_history(i, carry):
        hist_piece(order[0], i)
        return carry

    lax.fori_loop(0, pieces, first_history, 0)
    for off in range(1, slices):
        cand_copy(off).wait()

    def part_copy(off, h):
        there = other_slice(off)
        return pltpu.make_async_remote_copy(
            src_ref=parts.at[there, h],
            dst_ref=arrived.at[my_slice, h],
            send_sem=part_send.at[off, h],
            recv_sem=part_recv.at[off, h],
            device_id={"tm": there},
            device_id_type=MESH,
        )

    head_of = lax.broadcasted_iota(jnp.int32, (width, cand_block), 0) // head_dim
    lowest = jnp.full((8, cand_block), -jnp.inf, f32)
    steps = slice_len // ROW_STEP
    subs = capacity // SUB
    last = requests * items - 1

    def block_of(item):
        turn, j = item // items, item % items // HEADS
        r = lax.rem(my_slice // blocks + 1 + turn, requests)
        return r, r * blocks + lax.rem(my_slice + 1 + j, blocks)

    def one_block(n, carry):
        _, block = block_of(n * HEADS)
        query = jnp.dot(cands[block], w_query[...], preferred_element_type=f32)
        turned = query.astype(bf16).astype(f32).T
        for h in range(HEADS):
            qt[n * HEADS + h] = jnp.where(head_of == h, turned, 0.0).astype(bf16)
        return carry

    lax.fori_loop(0, slices, one_block, 0)

    def project_request(turn):
        r = order[turn]
        live = lengths[r] - my_slice * slice_len
        first_key = jnp.dot(found[r * pieces, 0:16, :], w_key[...], preferred_element_type=f32)[0:1]

        def project(i, c):
            rows = pl.ds(pl.multiple_of(i * capacity, capacity), capacity)
            x = found[r * pieces + i]
            key = jnp.dot(x, w_key[...], preferred_element_type=f32)
            down = lax.broadcasted_iota(jnp.int32, (capacity, width), 0) + i * capacity < live
            landing[turn * pieces + i] = jnp.where(down, key, first_key).astype(bf16)
            turned = lax.dot_general(
                w_value[...], x, (((0,), (1,)), ((), ())), preferred_element_type=f32
            )
            visible = lax.broadcasted_iota(jnp.int32, (1, capacity), 1) + i * capacity < live
            turned = jnp.where(visible, turned, 0.0).astype(bf16)
            first = lax.broadcasted_iota(jnp.int32, (16, capacity), 0) == 0
            ones = jnp.where(first, jnp.where(visible, 1.0, 0.0), 0.0).astype(bf16)
            for h in range(HEADS):
                at = turn * HEADS + h
                values[at, 0:head_dim, rows] = turned[h * head_dim : (h + 1) * head_dim]
                values[at, head_dim:HEAD_ROWS, rows] = ones
            return c

        lax.fori_loop(0, pieces, project, 0)

    def score(item, i, j):
        piece = item // items * pieces + i * (ROW_STEP // capacity) + j // subs
        keys = landing[piece, pl.ds(j % subs * SUB, SUB), :]
        return jnp.dot(keys, qt[item], preferred_element_type=f32)

    def raised(peak, s):
        return jnp.maximum(peak, jnp.max(s.reshape(SUB // 8, 8, cand_block), axis=0))

    def step_scores(i):
        return scores.at[pl.ds(pl.multiple_of(i * ROW_STEP, ROW_STEP), ROW_STEP)]

    def first_scores(i, peak):
        held = step_scores(i)
        for j in range(ROW_STEP // SUB):
            s = score(0, i, j)
            held[j * SUB : (j + 1) * SUB, :] = s
            peak = raised(peak, s)
        return peak

    def one_item(item, peak, beside=None, follow=True):
        top = jnp.max(peak, axis=0, keepdims=True)
        at = item // items * HEADS + item % HEADS

        def attend_step(i, c):
            next_peak, total = c
            held = step_scores(i)
            if beside is not None:
                beside(item * steps + i)
            for j in range(ROW_STEP // SUB):
                part = slice(j * SUB, (j + 1) * SUB)
                rows = pl.ds(pl.multiple_of(i * ROW_STEP + j * SUB, SUB), SUB)
                weights = jnp.exp2((held[part, :] - top) * to_exp2).astype(bf16)
                if follow:
                    s = score(item + 1, i, j)
                    held[part, :] = s
                    next_peak = raised(next_peak, s)
                total = total + jnp.dot(values[at, :, rows], weights, preferred_element_type=f32)
            return next_peak, total

        next_peak, total = lax.fori_loop(
            0, steps, attend_step, (lowest, jnp.zeros((HEAD_ROWS, cand_block), f32))
        )
        r, there = block_of(item)
        h = item % HEADS
        live = lengths[r] - my_slice * slice_len
        shown = jnp.where(live > 0, top * scale, NEG_FILL)
        row = lax.broadcasted_iota(jnp.int32, (8, cand_block), 0)
        tail = jnp.where(row == 1, shown, total[head_dim:PART_ROWS])

        @pl.when(there != my_slice)
        def _():
            parts[there, h, 0:head_dim, :] = total[0:head_dim]
            parts[there, h, head_dim:PART_ROWS, :] = tail
            part_copy(lax.rem(there - my_slice + slices, slices), h).start()

        @pl.when(there == my_slice)
        def _():
            arrived[my_slice, h, 0:head_dim, :] = total[0:head_dim]
            arrived[my_slice, h, head_dim:PART_ROWS, :] = tail

        return next_peak

    project_request(0)
    peak = lax.fori_loop(0, steps, first_scores, lowest)
    early = pieces // steps
    peak = lax.fori_loop(
        0, early, lambda n, p: one_item(n, p, beside=lambda i: hist_piece(order[1], i)), peak
    )
    project_request(1)
    peak = lax.fori_loop(early, last, one_item, peak)
    one_item(last, peak, follow=False)
    for off in range(1, slices):
        for h in range(HEADS):
            part_copy(off, h).wait()

    heads = []
    for h in range(HEADS):
        peaks = [arrived[s, h, head_dim + 1 : head_dim + 2, :] for s in range(slices)]
        best = functools.reduce(jnp.maximum, peaks)
        denom = numer = 0.0
        for s in range(slices):
            rescale = jnp.exp(peaks[s] - best)
            denom = denom + rescale * arrived[s, h, head_dim : head_dim + 1, :]
            numer = numer + rescale * arrived[s, h, 0:head_dim, :]
        heads.append(numer / denom)
    attended = jnp.concatenate(heads, axis=0).T.astype(bf16)
    out[...] = jnp.dot(attended, w_out[...], preferred_element_type=f32).astype(out.dtype)


def shards(
    table,
    fetch_rows,
    tile_counts,
    hist_source,
    cand_source,
    lengths,
    w_query,
    w_key,
    w_value,
    w_out,
):
    del tile_counts
    devices, capacity = fetch_rows.shape[2:]
    slice_len = hist_source.shape[3]
    cand_block = cand_source.shape[2]
    width = table.shape[1]
    slices, tiles = lax.axis_size("tm"), capacity // TILE
    requests = hist_source.shape[2]
    f32, bf16 = jnp.float32, jnp.bfloat16
    rows = (devices, capacity, width)
    part = (slices, HEADS, PART_ROWS, cand_block)
    dma = pltpu.SemaphoreType.DMA
    return pl.pallas_call(
        functools.partial(kernel, devices, slices),
        out_shape=jax.ShapeDtypeStruct((cand_block, w_out.shape[1]), bf16),
        in_specs=[SMEM] * 3 + [VMEM, ANY] + [VMEM] * 4,
        out_specs=VMEM,
        scratch_shapes=[
            pltpu.VMEM(table.shape, f32),
            pltpu.VMEM(rows, bf16),
            pltpu.VMEM(rows, bf16),
            pltpu.VMEM((slice_len, cand_block), f32),
            pltpu.VMEM((devices, tiles, TILE), jnp.int32),
            pltpu.SMEM((devices, tiles, TILE), jnp.int32),
            pltpu.VMEM((GATHER_STEP, width), f32),
            pltpu.VMEM((slices, cand_block, width), bf16),
            pltpu.VMEM((requests * HEADS, HEAD_ROWS, slice_len), bf16),
            pltpu.VMEM((slices * HEADS, width, cand_block), bf16),
            pltpu.VMEM(part, f32),
            pltpu.VMEM(part, f32),
            dma((TABLE_PIECES,)),
            dma,
            dma((devices,)),
            dma((devices,)),
            dma((devices,)),
            dma((devices,)),
            dma((slices,)),
            dma((slices,)),
            dma((slices, HEADS)),
            dma((slices, HEADS)),
        ],
        compiler_params=pltpu.CompilerParams(
            collective_id=1, has_side_effects=True, vmem_limit_bytes=VMEM_LIMIT
        ),
        name="attend",
    )(
        lengths[0],
        hist_source.reshape(-1, TILE),
        cand_source[0, 0],
        fetch_rows.reshape(devices, tiles, TILE),
        table.reshape(rows),
        w_query,
        w_key,
        w_value,
        w_out,
    )


def solution(mesh):
    return jax.shard_map(
        shards,
        mesh=mesh,
        in_specs=(
            P("tbl", None),
            P("tbl", "tm", None, None),
            P("tbl", "tm", None),
            P("tbl", "tm", None, None),
            P("tbl", "tm", None),
            P("tbl", None),
            P(),
            P(),
            P(),
            P(),
        ),
        out_specs=P(("tbl", "tm"), None),
        check_vma=False,
    )
```

```python
import functools
import math

import jax
import jax.numpy as jnp
from jax import lax
from jax.experimental import pallas as pl
from jax.experimental.pallas import tpu as pltpu
from jax.sharding import PartitionSpec as P

HEADS = 4
TILE = 128
HEAD_ROWS = 48
PART_ROWS = 40
ROW_STEP = 2048
SUB = 256
GATHER_STEP = 256
TABLE_PIECES = 8
ID_BATCHES = 4
STRIDE = 27
VMEM_LIMIT = 62 << 20
NEG_FILL = -1e30

VMEM = pl.BlockSpec(memory_space=pltpu.VMEM)
SMEM = pl.BlockSpec(memory_space=pltpu.SMEM)
ANY = pl.BlockSpec(memory_space=pl.ANY)
MESH = pl.DeviceIdType.MESH


def kernel(
    devices,
    slices,
    lengths,
    hist_source,
    cand_source,
    ids,
    table,
    w_query,
    w_key,
    w_value,
    w_out,
    out,
    wide,
    found,
    landing,
    scores,
    ids_landing,
    asked,
    rows_wide,
    cands,
    values,
    qt,
    parts,
    arrived,
    table_sem,
    asked_sem,
    ids_send,
    ids_recv,
    row_send,
    row_recv,
    cand_send,
    cand_recv,
    part_send,
    part_recv,
):
    f32, bf16 = jnp.float32, jnp.bfloat16
    me, my_slice = lax.axis_index("tbl"), lax.axis_index("tm")
    capacity, width = found.shape[1:]
    cand_block = cands.shape[1]
    requests, slice_len = lengths.shape[0], hist_source.size // lengths.shape[0]
    blocks = slices // requests
    items = blocks * HEADS
    head_dim = width // HEADS
    scale = 1.0 / math.sqrt(head_dim)
    to_exp2 = scale * math.log2(math.e)

    def forward(k):
        return lax.rem(me + k * STRIDE, devices)

    def backward(k):
        return lax.rem(me + k * (devices - STRIDE), devices)

    def other_slice(off):
        return lax.rem(my_slice + off, slices)

    per_piece = devices // TABLE_PIECES

    def table_copy(p):
        part = pl.ds(p * per_piece, per_piece)
        return pltpu.make_async_copy(table.at[part], found.at[part], table_sem.at[p])

    for p in range(TABLE_PIECES):
        table_copy(p).start()

    barrier = pltpu.get_barrier_semaphore()

    def greet(k, carry):
        pl.semaphore_signal(barrier, 1, device_id={"tbl": forward(k)}, device_id_type=MESH)
        return carry

    lax.fori_loop(1, devices, greet, 0)
    for off in range(1, slices):
        pl.semaphore_signal(barrier, 1, device_id={"tm": other_slice(off)}, device_id_type=MESH)
    pl.semaphore_wait(barrier, devices - 1 + slices - 1)

    def ids_copy(k):
        peer = backward(k)
        return pltpu.make_async_remote_copy(
            src_ref=ids.at[peer],
            dst_ref=ids_landing.at[k],
            send_sem=ids_send.at[k],
            recv_sem=ids_recv.at[k],
            device_id={"tbl": peer},
            device_id_type=MESH,
        )

    def send_ids(k, carry):
        ids_copy(k).start()
        return carry

    lax.fori_loop(1, devices, send_ids, 0)
    ids_landing[0] = ids[me]

    def widen(buffer, d):
        rows = pl.ds(pl.multiple_of(d * capacity, capacity), capacity)
        wide[rows, :] = buffer[d].astype(f32)

    for p in range(TABLE_PIECES):
        table_copy(p).wait()

        def widen_table(i, carry, p=p):
            widen(found, p * per_piece + i)
            return carry

        lax.fori_loop(0, per_piece, widen_table, 0)

    def wait_ids(k, carry):
        ids_copy(k).wait()
        return carry

    per_batch = devices // ID_BATCHES

    def list_copy(n):
        part = pl.ds(n * per_batch, per_batch)
        return pltpu.make_async_copy(ids_landing.at[part], asked.at[part], asked_sem.at[n])

    for n in range(ID_BATCHES):
        lax.fori_loop(max(1, n * per_batch), (n + 1) * per_batch, wait_ids, 0)
        list_copy(n).start()

    def look_up(k):
        def group(i, carry):
            for j in range(GATHER_STEP):
                row = asked[k, i * (GATHER_STEP // TILE) + j // TILE, j % TILE]
                rows_wide[j : j + 1, :] = wide[pl.ds(row, 1), :]
            rows = pl.ds(pl.multiple_of(i * GATHER_STEP, GATHER_STEP), GATHER_STEP)
            found[k, rows, :] = rows_wide[0:GATHER_STEP, :].astype(bf16)
            return carry

        lax.fori_loop(0, capacity // GATHER_STEP, group, 0)

    def row_copy(k):
        return pltpu.make_async_remote_copy(
            src_ref=found.at[k],
            dst_ref=landing.at[me],
            send_sem=row_send.at[k],
            recv_sem=row_recv.at[k],
            device_id={"tbl": forward(k)},
            device_id_type=MESH,
        )

    def send_rows(k, carry):
        look_up(k)
        row_copy(k).start()
        return carry

    for n in range(ID_BATCHES):
        list_copy(n).wait()
        lax.fori_loop(max(1, n * per_batch), (n + 1) * per_batch, send_rows, 0)
    look_up(0)
    own_rows = pl.ds(pl.multiple_of(me * capacity, capacity), capacity)
    wide[own_rows, :] = found[0].astype(f32)

    def take_rows(k, carry):
        row_copy(k).wait()
        widen(landing, backward(k))
        return carry

    lax.fori_loop(1, devices, take_rows, 0)

    def gather(pick):
        for j in range(GATHER_STEP):
            rows_wide[j : j + 1, :] = wide[pl.ds(pick(j), 1), :]
        return rows_wide[0:GATHER_STEP, :].astype(bf16)

    def cand_group(i, carry):
        base = pl.multiple_of(i * GATHER_STEP, GATHER_STEP)
        cands[my_slice, pl.ds(base, GATHER_STEP), :] = gather(lambda j: cand_source[base + j])
        return carry

    lax.fori_loop(0, cand_block // GATHER_STEP, cand_group, 0)

    def cand_copy(off):
        return pltpu.make_async_remote_copy(
            src_ref=cands.at[my_slice],
            dst_ref=cands.at[my_slice],
            send_sem=cand_send.at[off],
            recv_sem=cand_recv.at[off],
            device_id={"tm": other_slice(off)},
            device_id_type=MESH,
        )

    for off in range(1, slices):
        cand_copy(off).start()

    pieces = slice_len // capacity
    halves = capacity // GATHER_STEP
    order = [lax.rem(my_slice // blocks + 1 + turn, requests) for turn in range(requests)]

    def hist_piece(r, i):
        piece = r * pieces + i
        for half in range(halves):
            first = (piece * halves + half) * (GATHER_STEP // TILE)
            found[piece, half * GATHER_STEP : (half + 1) * GATHER_STEP, :] = gather(
                lambda j: hist_source[first + j // TILE, j % TILE]
            )

    def first_history(i, carry):
        hist_piece(order[0], i)
        return carry

    lax.fori_loop(0, pieces, first_history, 0)
    for off in range(1, slices):
        cand_copy(off).wait()

    def part_copy(off, h):
        there = other_slice(off)
        return pltpu.make_async_remote_copy(
            src_ref=parts.at[there, h],
            dst_ref=arrived.at[my_slice, h],
            send_sem=part_send.at[off, h],
            recv_sem=part_recv.at[off, h],
            device_id={"tm": there},
            device_id_type=MESH,
        )

    head_of = lax.broadcasted_iota(jnp.int32, (width, cand_block), 0) // head_dim
    lowest = jnp.full((8, cand_block), -jnp.inf, f32)
    steps = slice_len // ROW_STEP
    subs = capacity // SUB
    last = requests * items - 1

    def block_of(item):
        turn, j = item // items, item % items // HEADS
        r = lax.rem(my_slice // blocks + 1 + turn, requests)
        return r, r * blocks + lax.rem(my_slice + 1 + j, blocks)

    def one_block(n, carry):
        _, block = block_of(n * HEADS)
        query = jnp.dot(cands[block], w_query[...], preferred_element_type=f32)
        turned = query.astype(bf16).astype(f32).T
        for h in range(HEADS):
            qt[n * HEADS + h] = jnp.where(head_of == h, turned, 0.0).astype(bf16)
        return carry

    lax.fori_loop(0, slices, one_block, 0)

    def project_request(turn):
        r = order[turn]
        live = lengths[r] - my_slice * slice_len
        first_key = jnp.dot(found[r * pieces, 0:16, :], w_key[...], preferred_element_type=f32)[0:1]

        def project(i, c):
            rows = pl.ds(pl.multiple_of(i * capacity, capacity), capacity)
            x = found[r * pieces + i]
            key = jnp.dot(x, w_key[...], preferred_element_type=f32)
            down = lax.broadcasted_iota(jnp.int32, (capacity, width), 0) + i * capacity < live
            landing[turn * pieces + i] = jnp.where(down, key, first_key).astype(bf16)
            turned = lax.dot_general(
                w_value[...], x, (((0,), (1,)), ((), ())), preferred_element_type=f32
            )
            visible = lax.broadcasted_iota(jnp.int32, (1, capacity), 1) + i * capacity < live
            turned = jnp.where(visible, turned, 0.0).astype(bf16)
            first = lax.broadcasted_iota(jnp.int32, (16, capacity), 0) == 0
            ones = jnp.where(first, jnp.where(visible, 1.0, 0.0), 0.0).astype(bf16)
            for h in range(HEADS):
                at = turn * HEADS + h
                values[at, 0:head_dim, rows] = turned[h * head_dim : (h + 1) * head_dim]
                values[at, head_dim:HEAD_ROWS, rows] = ones
            return c

        lax.fori_loop(0, pieces, project, 0)

    def score(item, i, j):
        piece = item // items * pieces + i * (ROW_STEP // capacity) + j // subs
        keys = landing[piece, pl.ds(j % subs * SUB, SUB), :]
        return jnp.dot(keys, qt[item], preferred_element_type=f32)

    def raised(peak, s):
        return jnp.maximum(peak, jnp.max(s.reshape(SUB // 8, 8, cand_block), axis=0))

    def step_scores(i):
        return scores.at[pl.ds(pl.multiple_of(i * ROW_STEP, ROW_STEP), ROW_STEP)]

    def first_scores(i, peak):
        held = step_scores(i)
        for j in range(ROW_STEP // SUB):
            s = score(0, i, j)
            held[j * SUB : (j + 1) * SUB, :] = s
            peak = raised(peak, s)
        return peak

    def one_item(item, peak, beside=None, follow=True):
        top = jnp.max(peak, axis=0, keepdims=True)
        at = item // items * HEADS + item % HEADS

        def attend_step(i, c):
            next_peak, total = c
            held = step_scores(i)
            for j in range(ROW_STEP // SUB):
                if beside is not None:
                    beside(item * steps + i, j)
                part = slice(j * SUB, (j + 1) * SUB)
                rows = pl.ds(pl.multiple_of(i * ROW_STEP + j * SUB, SUB), SUB)
                weights = jnp.exp2((held[part, :] - top) * to_exp2).astype(bf16)
                if follow:
                    s = score(item + 1, i, j)
                    held[part, :] = s
                    next_peak = raised(next_peak, s)
                total = total + jnp.dot(values[at, :, rows], weights, preferred_element_type=f32)
            return next_peak, total

        next_peak, total = lax.fori_loop(
            0, steps, attend_step, (lowest, jnp.zeros((HEAD_ROWS, cand_block), f32))
        )
        r, there = block_of(item)
        h = item % HEADS
        live = lengths[r] - my_slice * slice_len
        shown = jnp.where(live > 0, top * scale, NEG_FILL)
        row = lax.broadcasted_iota(jnp.int32, (8, cand_block), 0)
        tail = jnp.where(row == 1, shown, total[head_dim:PART_ROWS])

        @pl.when(there != my_slice)
        def _():
            parts[there, h, 0:head_dim, :] = total[0:head_dim]
            parts[there, h, head_dim:PART_ROWS, :] = tail
            part_copy(lax.rem(there - my_slice + slices, slices), h).start()

        @pl.when(there == my_slice)
        def _():
            arrived[my_slice, h, 0:head_dim, :] = total[0:head_dim]
            arrived[my_slice, h, head_dim:PART_ROWS, :] = tail

        return next_peak

    project_request(0)
    peak = lax.fori_loop(0, steps, first_scores, lowest)
    early = pieces // steps
    few = capacity // (ROW_STEP // SUB)

    def gather_few(i, j):
        piece = order[1] * pieces + i
        part = slice(j * few, (j + 1) * few)
        for n in range(j * few, (j + 1) * few):
            row = hist_source[piece * (capacity // TILE) + n // TILE, n % TILE]
            rows_wide[n : n + 1, :] = wide[pl.ds(row, 1), :]
        found[piece, part, :] = rows_wide[part, :].astype(bf16)

    peak = lax.fori_loop(0, early, lambda n, p: one_item(n, p, beside=gather_few), peak)
    project_request(1)
    peak = lax.fori_loop(early, last, one_item, peak)
    one_item(last, peak, follow=False)
    for off in range(1, slices):
        for h in range(HEADS):
            part_copy(off, h).wait()

    heads = []
    for h in range(HEADS):
        peaks = [arrived[s, h, head_dim + 1 : head_dim + 2, :] for s in range(slices)]
        best = functools.reduce(jnp.maximum, peaks)
        denom = numer = 0.0
        for s in range(slices):
            rescale = jnp.exp(peaks[s] - best)
            denom = denom + rescale * arrived[s, h, head_dim : head_dim + 1, :]
            numer = numer + rescale * arrived[s, h, 0:head_dim, :]
        heads.append(numer / denom)
    attended = jnp.concatenate(heads, axis=0).T.astype(bf16)
    out[...] = jnp.dot(attended, w_out[...], preferred_element_type=f32).astype(out.dtype)


def shards(
    table,
    fetch_rows,
    tile_counts,
    hist_source,
    cand_source,
    lengths,
    w_query,
    w_key,
    w_value,
    w_out,
):
    del tile_counts
    devices, capacity = fetch_rows.shape[2:]
    slice_len = hist_source.shape[3]
    cand_block = cand_source.shape[2]
    width = table.shape[1]
    slices, tiles = lax.axis_size("tm"), capacity // TILE
    requests = hist_source.shape[2]
    f32, bf16 = jnp.float32, jnp.bfloat16
    rows = (devices, capacity, width)
    part = (slices, HEADS, PART_ROWS, cand_block)
    dma = pltpu.SemaphoreType.DMA
    return pl.pallas_call(
        functools.partial(kernel, devices, slices),
        out_shape=jax.ShapeDtypeStruct((cand_block, w_out.shape[1]), bf16),
        in_specs=[SMEM] * 3 + [VMEM, ANY] + [VMEM] * 4,
        out_specs=VMEM,
        scratch_shapes=[
            pltpu.VMEM(table.shape, f32),
            pltpu.VMEM(rows, bf16),
            pltpu.VMEM(rows, bf16),
            pltpu.VMEM((slice_len, cand_block), f32),
            pltpu.VMEM((devices, tiles, TILE), jnp.int32),
            pltpu.SMEM((devices, tiles, TILE), jnp.int32),
            pltpu.VMEM((capacity, width), f32),
            pltpu.VMEM((slices, cand_block, width), bf16),
            pltpu.VMEM((requests * HEADS, HEAD_ROWS, slice_len), bf16),
            pltpu.VMEM((slices * HEADS, width, cand_block), bf16),
            pltpu.VMEM(part, f32),
            pltpu.VMEM(part, f32),
            dma((TABLE_PIECES,)),
            dma((ID_BATCHES,)),
            dma((devices,)),
            dma((devices,)),
            dma((devices,)),
            dma((devices,)),
            dma((slices,)),
            dma((slices,)),
            dma((slices, HEADS)),
            dma((slices, HEADS)),
        ],
        compiler_params=pltpu.CompilerParams(
            collective_id=1, has_side_effects=True, vmem_limit_bytes=VMEM_LIMIT
        ),
        name="attend",
    )(
        lengths[0],
        hist_source.reshape(-1, TILE),
        cand_source[0, 0],
        fetch_rows.reshape(devices, tiles, TILE),
        table.reshape(rows),
        w_query,
        w_key,
        w_value,
        w_out,
    )


def solution(mesh):
    return jax.shard_map(
        shards,
        mesh=mesh,
        in_specs=(
            P("tbl", None),
            P("tbl", "tm", None, None),
            P("tbl", "tm", None),
            P("tbl", "tm", None, None),
            P("tbl", "tm", None),
            P("tbl", None),
            P(),
            P(),
            P(),
            P(),
        ),
        out_specs=P(("tbl", "tm"), None),
        check_vma=False,
    )
```

```python
import functools
import math

import jax
import jax.numpy as jnp
from jax import lax
from jax.experimental import pallas as pl
from jax.experimental.pallas import tpu as pltpu
from jax.sharding import PartitionSpec as P

HEADS = 4
TILE = 128
HEAD_ROWS = 48
PART_ROWS = 40
ROW_STEP = 4096
BESIDE = 64
SUB = 256
GATHER_STEP = 256
TABLE_PIECES = 8
ID_BATCHES = 4
STRIDE = 27
VMEM_LIMIT = 62 << 20
NEG_FILL = -1e30

VMEM = pl.BlockSpec(memory_space=pltpu.VMEM)
SMEM = pl.BlockSpec(memory_space=pltpu.SMEM)
ANY = pl.BlockSpec(memory_space=pl.ANY)
MESH = pl.DeviceIdType.MESH


def kernel(
    devices,
    slices,
    lengths,
    hist_source,
    cand_source,
    ids,
    table,
    w_query,
    w_key,
    w_value,
    w_out,
    out,
    wide,
    found,
    landing,
    scores,
    ids_landing,
    asked,
    rows_wide,
    cands,
    values,
    qt,
    parts,
    arrived,
    table_sem,
    asked_sem,
    ids_send,
    ids_recv,
    row_send,
    row_recv,
    cand_send,
    cand_recv,
    part_send,
    part_recv,
):
    f32, bf16 = jnp.float32, jnp.bfloat16
    me, my_slice = lax.axis_index("tbl"), lax.axis_index("tm")
    capacity, width = found.shape[1:]
    cand_block = cands.shape[1]
    requests, slice_len = lengths.shape[0], hist_source.size // lengths.shape[0]
    blocks = slices // requests
    items = blocks * HEADS
    head_dim = width // HEADS
    scale = 1.0 / math.sqrt(head_dim)
    to_exp2 = scale * math.log2(math.e)

    def forward(k):
        return lax.rem(me + k * STRIDE, devices)

    def backward(k):
        return lax.rem(me + k * (devices - STRIDE), devices)

    def other_slice(off):
        return lax.rem(my_slice + off, slices)

    per_piece = devices // TABLE_PIECES

    def table_copy(p):
        part = pl.ds(p * per_piece, per_piece)
        return pltpu.make_async_copy(table.at[part], found.at[part], table_sem.at[p])

    for p in range(TABLE_PIECES):
        table_copy(p).start()

    barrier = pltpu.get_barrier_semaphore()

    def greet(k, carry):
        pl.semaphore_signal(barrier, 1, device_id={"tbl": forward(k)}, device_id_type=MESH)
        return carry

    lax.fori_loop(1, devices, greet, 0)
    for off in range(1, slices):
        pl.semaphore_signal(barrier, 1, device_id={"tm": other_slice(off)}, device_id_type=MESH)
    pl.semaphore_wait(barrier, devices - 1 + slices - 1)

    def ids_copy(k):
        peer = backward(k)
        return pltpu.make_async_remote_copy(
            src_ref=ids.at[peer],
            dst_ref=ids_landing.at[k],
            send_sem=ids_send.at[k],
            recv_sem=ids_recv.at[k],
            device_id={"tbl": peer},
            device_id_type=MESH,
        )

    def send_ids(k, carry):
        ids_copy(k).start()
        return carry

    lax.fori_loop(1, devices, send_ids, 0)
    ids_landing[0] = ids[me]

    def widen(buffer, d):
        rows = pl.ds(pl.multiple_of(d * capacity, capacity), capacity)
        wide[rows, :] = buffer[d].astype(f32)

    for p in range(TABLE_PIECES):
        table_copy(p).wait()

        def widen_table(i, carry, p=p):
            widen(found, p * per_piece + i)
            return carry

        lax.fori_loop(0, per_piece, widen_table, 0)

    def wait_ids(k, carry):
        ids_copy(k).wait()
        return carry

    per_batch = devices // ID_BATCHES

    def list_copy(n):
        part = pl.ds(n * per_batch, per_batch)
        return pltpu.make_async_copy(ids_landing.at[part], asked.at[part], asked_sem.at[n])

    for n in range(ID_BATCHES):
        lax.fori_loop(max(1, n * per_batch), (n + 1) * per_batch, wait_ids, 0)
        list_copy(n).start()

    def look_up(k):
        def group(i, carry):
            for j in range(GATHER_STEP):
                row = asked[k, i * (GATHER_STEP // TILE) + j // TILE, j % TILE]
                rows_wide[j : j + 1, :] = wide[pl.ds(row, 1), :]
            rows = pl.ds(pl.multiple_of(i * GATHER_STEP, GATHER_STEP), GATHER_STEP)
            found[k, rows, :] = rows_wide[0:GATHER_STEP, :].astype(bf16)
            return carry

        lax.fori_loop(0, capacity // GATHER_STEP, group, 0)

    def row_copy(k):
        return pltpu.make_async_remote_copy(
            src_ref=found.at[k],
            dst_ref=landing.at[me],
            send_sem=row_send.at[k],
            recv_sem=row_recv.at[k],
            device_id={"tbl": forward(k)},
            device_id_type=MESH,
        )

    def send_rows(k, carry):
        look_up(k)
        row_copy(k).start()
        return carry

    for n in range(ID_BATCHES):
        list_copy(n).wait()
        lax.fori_loop(max(1, n * per_batch), (n + 1) * per_batch, send_rows, 0)
    look_up(0)
    own_rows = pl.ds(pl.multiple_of(me * capacity, capacity), capacity)
    wide[own_rows, :] = found[0].astype(f32)

    def take_rows(k, carry):
        row_copy(k).wait()
        widen(landing, backward(k))
        return carry

    lax.fori_loop(1, devices, take_rows, 0)

    def gather(pick):
        for j in range(GATHER_STEP):
            rows_wide[j : j + 1, :] = wide[pl.ds(pick(j), 1), :]
        return rows_wide[0:GATHER_STEP, :].astype(bf16)

    def cand_group(i, carry):
        base = pl.multiple_of(i * GATHER_STEP, GATHER_STEP)
        cands[my_slice, pl.ds(base, GATHER_STEP), :] = gather(lambda j: cand_source[base + j])
        return carry

    lax.fori_loop(0, cand_block // GATHER_STEP, cand_group, 0)

    def cand_copy(off):
        return pltpu.make_async_remote_copy(
            src_ref=cands.at[my_slice],
            dst_ref=cands.at[my_slice],
            send_sem=cand_send.at[off],
            recv_sem=cand_recv.at[off],
            device_id={"tm": other_slice(off)},
            device_id_type=MESH,
        )

    for off in range(1, slices):
        cand_copy(off).start()

    pieces = slice_len // capacity
    halves = capacity // GATHER_STEP
    order = [lax.rem(my_slice // blocks + 1 + turn, requests) for turn in range(requests)]

    def hist_piece(r, i):
        piece = r * pieces + i
        for half in range(halves):
            first = (piece * halves + half) * (GATHER_STEP // TILE)
            found[piece, half * GATHER_STEP : (half + 1) * GATHER_STEP, :] = gather(
                lambda j: hist_source[first + j // TILE, j % TILE]
            )

    def first_history(i, carry):
        hist_piece(order[0], i)
        return carry

    lax.fori_loop(0, pieces, first_history, 0)
    for off in range(1, slices):
        cand_copy(off).wait()

    def part_copy(off, h):
        there = other_slice(off)
        return pltpu.make_async_remote_copy(
            src_ref=parts.at[there, h],
            dst_ref=arrived.at[my_slice, h],
            send_sem=part_send.at[off, h],
            recv_sem=part_recv.at[off, h],
            device_id={"tm": there},
            device_id_type=MESH,
        )

    head_of = lax.broadcasted_iota(jnp.int32, (width, cand_block), 0) // head_dim
    lowest = jnp.full((8, cand_block), -jnp.inf, f32)
    steps = slice_len // ROW_STEP
    subs = capacity // SUB
    last = requests * items - 1

    def block_of(item):
        turn, j = item // items, item % items // HEADS
        r = lax.rem(my_slice // blocks + 1 + turn, requests)
        return r, r * blocks + lax.rem(my_slice + 1 + j, blocks)

    def one_block(n, carry):
        _, block = block_of(n * HEADS)
        query = jnp.dot(cands[block], w_query[...], preferred_element_type=f32)
        turned = query.astype(bf16).astype(f32).T
        for h in range(HEADS):
            qt[n * HEADS + h] = jnp.where(head_of == h, turned, 0.0).astype(bf16)
        return carry

    lax.fori_loop(0, slices, one_block, 0)

    def project_request(turn):
        r = order[turn]
        live = lengths[r] - my_slice * slice_len
        first_key = jnp.dot(found[r * pieces, 0:16, :], w_key[...], preferred_element_type=f32)[0:1]

        def project(i, c):
            rows = pl.ds(pl.multiple_of(i * capacity, capacity), capacity)
            x = found[r * pieces + i]
            key = jnp.dot(x, w_key[...], preferred_element_type=f32)
            down = lax.broadcasted_iota(jnp.int32, (capacity, width), 0) + i * capacity < live
            landing[turn * pieces + i] = jnp.where(down, key, first_key).astype(bf16)
            turned = lax.dot_general(
                w_value[...], x, (((0,), (1,)), ((), ())), preferred_element_type=f32
            )
            visible = lax.broadcasted_iota(jnp.int32, (1, capacity), 1) + i * capacity < live
            turned = jnp.where(visible, turned, 0.0).astype(bf16)
            first = lax.broadcasted_iota(jnp.int32, (16, capacity), 0) == 0
            ones = jnp.where(first, jnp.where(visible, 1.0, 0.0), 0.0).astype(bf16)
            for h in range(HEADS):
                at = turn * HEADS + h
                values[at, 0:head_dim, rows] = turned[h * head_dim : (h + 1) * head_dim]
                values[at, head_dim:HEAD_ROWS, rows] = ones
            return c

        lax.fori_loop(0, pieces, project, 0)

    def score(item, i, j):
        piece = item // items * pieces + i * (ROW_STEP // capacity) + j // subs
        keys = landing[piece, pl.ds(j % subs * SUB, SUB), :]
        return jnp.dot(keys, qt[item], preferred_element_type=f32)

    def raised(peak, s):
        return jnp.maximum(peak, jnp.max(s.reshape(SUB // 8, 8, cand_block), axis=0))

    def step_scores(i):
        return scores.at[pl.ds(pl.multiple_of(i * ROW_STEP, ROW_STEP), ROW_STEP)]

    def first_scores(i, peak):
        held = step_scores(i)
        for j in range(ROW_STEP // SUB):
            s = score(0, i, j)
            held[j * SUB : (j + 1) * SUB, :] = s
            peak = raised(peak, s)
        return peak

    def one_item(item, peak, beside=None, follow=True):
        top = jnp.max(peak, axis=0, keepdims=True)
        at = item // items * HEADS + item % HEADS

        def attend_step(i, c):
            next_peak, total = c
            held = step_scores(i)
            for j in range(ROW_STEP // SUB):
                if beside is not None:
                    beside(item * steps + i, j)
                part = slice(j * SUB, (j + 1) * SUB)
                rows = pl.ds(pl.multiple_of(i * ROW_STEP + j * SUB, SUB), SUB)
                weights = jnp.exp2((held[part, :] - top) * to_exp2).astype(bf16)
                if follow:
                    s = score(item + 1, i, j)
                    held[part, :] = s
                    next_peak = raised(next_peak, s)
                total = total + jnp.dot(values[at, :, rows], weights, preferred_element_type=f32)
            return next_peak, total

        next_peak, total = lax.fori_loop(
            0, steps, attend_step, (lowest, jnp.zeros((HEAD_ROWS, cand_block), f32))
        )
        r, there = block_of(item)
        h = item % HEADS
        live = lengths[r] - my_slice * slice_len
        shown = jnp.where(live > 0, top * scale, NEG_FILL)
        row = lax.broadcasted_iota(jnp.int32, (8, cand_block), 0)
        tail = jnp.where(row == 1, shown, total[head_dim:PART_ROWS])

        @pl.when(there != my_slice)
        def _():
            parts[there, h, 0:head_dim, :] = total[0:head_dim]
            parts[there, h, head_dim:PART_ROWS, :] = tail
            part_copy(lax.rem(there - my_slice + slices, slices), h).start()

        @pl.when(there == my_slice)
        def _():
            arrived[my_slice, h, 0:head_dim, :] = total[0:head_dim]
            arrived[my_slice, h, head_dim:PART_ROWS, :] = tail

        return next_peak

    project_request(0)
    peak = lax.fori_loop(0, steps, first_scores, lowest)
    shares = capacity // BESIDE
    per_step = ROW_STEP // SUB // shares
    early = pieces // steps // per_step

    def gather_few(i, j):
        piece = order[1] * pieces + i * per_step + j // shares
        start = j % shares * BESIDE
        for n in range(start, start + BESIDE):
            row = hist_source[piece * (capacity // TILE) + n // TILE, n % TILE]
            rows_wide[n : n + 1, :] = wide[pl.ds(row, 1), :]
        part = slice(start, start + BESIDE)
        found[piece, part, :] = rows_wide[part, :].astype(bf16)

    peak = lax.fori_loop(0, early, lambda n, p: one_item(n, p, beside=gather_few), peak)
    project_request(1)
    peak = lax.fori_loop(early, last, one_item, peak)
    one_item(last, peak, follow=False)
    for off in range(1, slices):
        for h in range(HEADS):
            part_copy(off, h).wait()

    heads = []
    for h in range(HEADS):
        peaks = [arrived[s, h, head_dim + 1 : head_dim + 2, :] for s in range(slices)]
        best = functools.reduce(jnp.maximum, peaks)
        denom = numer = 0.0
        for s in range(slices):
            rescale = jnp.exp(peaks[s] - best)
            denom = denom + rescale * arrived[s, h, head_dim : head_dim + 1, :]
            numer = numer + rescale * arrived[s, h, 0:head_dim, :]
        heads.append(numer / denom)
    attended = jnp.concatenate(heads, axis=0).T.astype(bf16)
    out[...] = jnp.dot(attended, w_out[...], preferred_element_type=f32).astype(out.dtype)


def shards(
    table,
    fetch_rows,
    tile_counts,
    hist_source,
    cand_source,
    lengths,
    w_query,
    w_key,
    w_value,
    w_out,
):
    del tile_counts
    devices, capacity = fetch_rows.shape[2:]
    slice_len = hist_source.shape[3]
    cand_block = cand_source.shape[2]
    width = table.shape[1]
    slices, tiles = lax.axis_size("tm"), capacity // TILE
    requests = hist_source.shape[2]
    f32, bf16 = jnp.float32, jnp.bfloat16
    rows = (devices, capacity, width)
    part = (slices, HEADS, PART_ROWS, cand_block)
    dma = pltpu.SemaphoreType.DMA
    return pl.pallas_call(
        functools.partial(kernel, devices, slices),
        out_shape=jax.ShapeDtypeStruct((cand_block, w_out.shape[1]), bf16),
        in_specs=[SMEM] * 3 + [VMEM, ANY] + [VMEM] * 4,
        out_specs=VMEM,
        scratch_shapes=[
            pltpu.VMEM(table.shape, f32),
            pltpu.VMEM(rows, bf16),
            pltpu.VMEM(rows, bf16),
            pltpu.VMEM((slice_len, cand_block), f32),
            pltpu.VMEM((devices, tiles, TILE), jnp.int32),
            pltpu.SMEM((devices, tiles, TILE), jnp.int32),
            pltpu.VMEM((capacity, width), f32),
            pltpu.VMEM((slices, cand_block, width), bf16),
            pltpu.VMEM((requests * HEADS, HEAD_ROWS, slice_len), bf16),
            pltpu.VMEM((slices * HEADS, width, cand_block), bf16),
            pltpu.VMEM(part, f32),
            pltpu.VMEM(part, f32),
            dma((TABLE_PIECES,)),
            dma((ID_BATCHES,)),
            dma((devices,)),
            dma((devices,)),
            dma((devices,)),
            dma((devices,)),
            dma((slices,)),
            dma((slices,)),
            dma((slices, HEADS)),
            dma((slices, HEADS)),
        ],
        compiler_params=pltpu.CompilerParams(
            collective_id=1, has_side_effects=True, vmem_limit_bytes=VMEM_LIMIT
        ),
        name="attend",
    )(
        lengths[0],
        hist_source.reshape(-1, TILE),
        cand_source[0, 0],
        fetch_rows.reshape(devices, tiles, TILE),
        table.reshape(rows),
        w_query,
        w_key,
        w_value,
        w_out,
    )


def solution(mesh):
    return jax.shard_map(
        shards,
        mesh=mesh,
        in_specs=(
            P("tbl", None),
            P("tbl", "tm", None, None),
            P("tbl", "tm", None),
            P("tbl", "tm", None, None),
            P("tbl", "tm", None),
            P("tbl", None),
            P(),
            P(),
            P(),
            P(),
        ),
        out_specs=P(("tbl", "tm"), None),
        check_vma=False,
    )
```
